768 devices in a mesh: row: 8 (over y), col: 24 (over z, core), inner: 4 (over x).
Axes of the slice: x: 4, y: 8, z: 12, core: 2. Of those that a mesh axis runs over, the one named last changes fastest.
Arguments:
- pattern: int32 [1536, 7], P(('row', 'col', 'inner')), may hold values from 0 to 1, as said below
- density: bfloat16 [1536, 7, 128, 128], P(('row', 'col', 'inner')), may hold values from -0.25 to 1.25, as said below
Outputs:
- purified: bfloat16 [1536, 7, 128, 128], P(('row', 'col', 'inner'))
- occupation: float32 [2], replicated
The draws below stay inside these ranges and needn't reach their ends.
Inputs may be any that keep to these rules, and one draw needn't show every extreme that they name: pattern[i, 3] is 1; pattern[i, s] is 0 where block column i + s - 3 lies outside the matrix; pattern is symmetric: pattern[i, s] = pattern[i + s - 3, 6 - s]. density is symmetric as a matrix and its blocks are zero where pattern is 0.
All inputs are finite; a program needn't handle non-finite values.
Results may differ from the reference program's by a relative error of at most 0.02.
Values may be sent and summed in bfloat16 or wider, within the bound.
A program may use at most 32 MiB of HBM per device.

```python
import math
import jax
import jax.numpy as jnp
from jax import lax

BLK = 128
REACH = 3
STEPS = 2
SLOTS = 7
NB = 1536
ORDER = 196608


def pattern_common(key):
    break_key = jax.random.fold_in(key, 11)
    reach_key = jax.random.fold_in(key, 13)
    starts = (jax.random.randint(break_key, (NB,), 0, 12) == 0).astype(jnp.int32)
    cluster = jnp.cumsum(starts)
    table = jax.random.randint(reach_key, (NB + 1,), 0, REACH + 1)
    places = jnp.arange(NB, dtype=jnp.int32)
    reach = jnp.where(places <= 2 * REACH, REACH, table[cluster])
    offsets = jnp.arange(2 * REACH + 1, dtype=jnp.int32) - REACH
    partner = places[:, None] + offsets[None, :]
    inside = (partner >= 0) & (partner < NB)
    reach_partner = reach[jnp.clip(partner, 0, NB - 1)]
    within = jnp.abs(offsets)[None, :] <= jnp.maximum(reach[:, None], reach_partner)
    return (inside & within).astype(jnp.int32)


def draw_pattern(key, part):
    return pattern_common(key)


def draw_density(key, part):
    blocks = pattern_common(key)
    noise_key = jax.random.fold_in(key, 23)
    filled_key = jax.random.fold_in(key, 29)
    jitter_key = jax.random.fold_in(key, 31)
    spread = 0.4 / math.sqrt(SLOTS * BLK)
    noise = jax.random.truncated_normal(noise_key, -4.0, 4.0, (NB, SLOTS, BLK, BLK), jnp.float32)
    filling = 0.125
    mirrored = jnp.stack([jnp.roll(noise[:, 2 * REACH - slot], -(slot - REACH), axis=0) for slot in range(SLOTS)], axis=1)
    symmetric = (noise + jnp.swapaxes(mirrored, 2, 3)) * (spread / math.sqrt(2.0))
    position = (jnp.arange(NB, dtype=jnp.float32) + 0.5) / NB
    chance = filling * (0.5 + position)
    filled = jax.random.uniform(filled_key, (NB,), jnp.float32) < chance
    level = jnp.where(filled, 0.88, 0.06)
    jitter = jax.random.uniform(jitter_key, (NB, BLK), jnp.float32, -0.03, 0.03)
    ladder = level[:, None] + jitter
    diagonal_blocks = ladder[:, :, None] * jnp.eye(BLK, dtype=jnp.float32)[None]
    centre = (jnp.arange(SLOTS) == REACH)[None, :, None, None]
    result = jnp.where(blocks[:, :, None, None] == 1, symmetric, 0.0) + jnp.where(centre, diagonal_blocks[:, None], 0.0)
    return result.astype(jnp.bfloat16)


def setup_inputs(seed: int = 0) -> dict:
    splits = jax.random.split(jax.random.key(seed), 3)
    return {
        "pattern": draw_pattern(jax.random.fold_in(splits[2], 71), 0),
        "density": draw_density(jax.random.fold_in(splits[2], 71), 0),
    }


def rows_at(band, offset):
    depth = 2 * REACH
    padded = jnp.pad(band, ((depth, depth), (0, 0), (0, 0)))
    return lax.slice_in_dim(padded, depth + offset, depth + offset + band.shape[0], axis=0)


def product(left, right):
    return jnp.einsum("irc,icd->ird", left.astype(jnp.float32), right.astype(jnp.float32))


def reference(pattern, density):
    kept = pattern == 1
    current = density
    traces = []
    for section in range(STEPS):
        square = []
        for target in range(4 * REACH + 1):
            total = jnp.zeros((NB, BLK, BLK), jnp.float32)
            for first in range(max(0, target - 2 * REACH), min(2 * REACH, target) + 1):
                total = total + product(current[:, first], rows_at(current[:, target - first], first - REACH))
            square.append(total.astype(jnp.bfloat16))
        columns = []
        for column in range(2 * REACH + 1):
            total = jnp.zeros((NB, BLK, BLK), jnp.float32)
            for middle in range(column, column + 2 * REACH + 1):
                total = total + product(square[middle], rows_at(current[:, column - middle + 2 * REACH], middle - 2 * REACH))
            value = 3.0 * square[column + REACH].astype(jnp.float32) - 2.0 * total
            columns.append(jnp.where(kept[:, column, None, None], value, 0.0).astype(jnp.bfloat16))
        updated = jnp.stack(columns, axis=1)
        traces.append(jnp.sum(jnp.diagonal(updated[:, REACH], axis1=1, axis2=2).astype(jnp.float32)) / ORDER)
        current = updated
    return current, jnp.stack(traces)
```

```python
import functools

import jax
import jax.numpy as jnp
from jax import lax
from jax.experimental import pallas as pl
from jax.experimental.pallas import tpu as pltpu
from jax.sharding import PartitionSpec as P

BLK = 128
REACH = 3
SLOTS = 7
STEPS = 2
CORES = 2
MESH = pl.DeviceIdType.MESH

WINDOW = 8
COLUMNS = WINDOW + SLOTS - 1

MESSAGES = (
    (4, 0, 4, 2, 1, None),
    (3, 3, 4, 5, -1, None),
    (3, 0, 4, 1, 1, None),
    (4, 3, 4, 6, -1, None),
    (4, 6, 1, 2, 1, None),
    (2, 0, 4, 0, 1, 0),
    (5, 3, 4, 7, -1, 1),
)
FROM_OWN = ((0, 6), (1, 5), (1, 6), (2, 4), (2, 5), (5, 1), (5, 2), (6, 0), (6, 1), (7, 0))
FROM_MESSAGE = {0: ((0, 5), (1, 4)), 1: ((6, 2), (7, 1)), 2: ((0, 4),), 3: ((7, 2),), 4: ((5, 0),)}


def kernel(
    sizes, pattern, density, purified, occupation, near0, near1, left, total, square, last,
    diagonals, sums_a, sums_b, sums_c, send_sem, recv_sem, load_sem, store_sem,
    sum_send, recv_a, recv_b, recv_c,
):
    rows, columns, inners = sizes
    count = rows * columns * inners
    row, col, inner = lax.axis_index("row"), lax.axis_index("col"), lax.axis_index("inner")
    place = (row * columns + col) * inners + inner

    def along(steps):
        other = lax.rem(place + steps + count, count)
        upper = other // inners
        return (upper // columns, lax.rem(upper, columns), lax.rem(other, inners))

    layers = columns // CORES
    layer, core = col // CORES, lax.rem(col, CORES)
    chip = core * inners + inner

    def partner_a(step):
        other = lax.rem(chip + step, CORES * inners)
        return (row, layer * CORES + other // inners, lax.rem(other, inners))

    def partner_b(step):
        return (row, lax.rem(layer + step, layers) * CORES + core, inner)

    def partner_c(step):
        return (lax.rem(row + step, rows), col, inner)

    phases = (
        (CORES * inners, chip, partner_a, sums_a, recv_a, 0),
        (layers, layer, partner_b, sums_b, recv_b, CORES * inners),
        (rows, row, partner_c, sums_c, recv_c, CORES * inners + layers),
    )

    load = pltpu.make_async_copy(density, near0.at[pl.ds(3, 2)], load_sem)
    load.start()

    barrier = pltpu.get_barrier_semaphore()
    greeted = 0
    for steps in (1, -1):
        pl.semaphore_signal(barrier, inc=1, device_id=along(steps), device_id_type=MESH)
        greeted += 1
    for size, _, partner, _, _, _ in phases:
        for step in range(1, size):
            pl.semaphore_signal(barrier, inc=1, device_id=partner(step), device_id_type=MESH)
            greeted += 1
    zero_block = jnp.zeros((BLK, BLK), jnp.bfloat16)
    left[0:BLK, 7 * BLK : 8 * BLK] = zero_block
    left[BLK : 2 * BLK, 0:BLK] = zero_block
    load.wait()
    pl.semaphore_wait(barrier, greeted)

    eye = lax.broadcasted_iota(jnp.int32, (BLK, BLK), 0) == lax.broadcasted_iota(jnp.int32, (BLK, BLK), 1)

    def block(near, r, column):
        slot = column - r
        return near[r, slot] if 0 <= slot < SLOTS else zero_block

    def tile(near, r, column, width):
        return jnp.concatenate(
            [
                jnp.concatenate([block(near, r + i, column + j) for j in range(width)], axis=1)
                for i in range(2)
            ],
            axis=0,
        )

    def mirror(near, places):
        for r, slot in places:
            near[r, slot] = near[r + slot - REACH, 2 * REACH - slot].T

    def span(column, width=2):
        return slice(column * BLK, (column + width) * BLK)

    def update(near, q, store):
        right = tile(near, 2 * q, 2 * q, 8)
        cube = lax.dot_general(
            square[:, span(2 * q, 8)], right, (((1,), (1,)), ((), ())), preferred_element_type=jnp.float32
        )
        for r in range(2):
            for j in range(2):
                slot = 2 * q + j - r
                if 0 <= slot < SLOTS:
                    mine = slice(r * BLK, (r + 1) * BLK)
                    value = (
                        3.0 * square[mine, span(2 * q + j + REACH, 1)].astype(jnp.float32)
                        - 2.0 * cube[mine, span(j, 1)]
                    )
                    store(r, slot, jnp.where(pattern[r, slot] == 1, value, 0.0).astype(jnp.bfloat16))

    def exchange(section, near):
        copies = []
        for index, (r, slot, slots, target, direction, after) in enumerate(MESSAGES):
            copies.append(
                pltpu.make_async_remote_copy(
                    src_ref=near.at[r, pl.ds(slot, slots)],
                    dst_ref=near.at[target, pl.ds(slot, slots)],
                    send_sem=send_sem.at[section, index],
                    recv_sem=recv_sem.at[section, index],
                    device_id=along(direction),
                    device_id_type=MESH,
                )
            )
            if after is None:
                copies[-1].start()
        return copies

    def squares(near, copies):
        for r in range(2):
            for slot in range(SLOTS):
                left[r * BLK : (r + 1) * BLK, span(slot + r, 1)] = near[3 + r, slot]
        mirror(near, FROM_OWN)
        copies[0].wait_recv()
        copies[5].start()
        copies[1].wait_recv()
        copies[6].start()
        mirror(near, FROM_MESSAGE[0])
        mirror(near, FROM_MESSAGE[1])
        copies[4].wait_recv()
        mirror(near, FROM_MESSAGE[4])
        for column in range(2, 12, 2):
            terms = [
                jnp.dot(left[:, span(r)], tile(near, r, column, 2), preferred_element_type=jnp.float32)
                for r in (2, 4)
                if r - 1 <= column <= r + 7
            ]
            total[:, span(column)] = functools.reduce(jnp.add, terms)
        copies[2].wait_recv()
        copies[3].wait_recv()
        mirror(near, FROM_MESSAGE[2])
        mirror(near, FROM_MESSAGE[3])
        copies[5].wait_recv()
        copies[6].wait_recv()
        for column in range(0, COLUMNS, 2):
            terms = [total[:, span(column)]] if 2 <= column < 12 else []
            terms += [
                jnp.dot(left[:, span(r)], tile(near, r, column, 2), preferred_element_type=jnp.float32)
                for r in (0, 6)
                if r - 1 <= column <= r + 7
            ]
            square[:, span(column)] = functools.reduce(jnp.add, terms).astype(jnp.bfloat16)

    copies0 = exchange(0, near0)
    squares(near0, copies0)

    def keep(r, slot, value):
        near1[3 + r, slot] = value

    for q in range(4):
        update(near0, q, keep)
    copies1 = exchange(1, near1)

    on_diagonal = sum(
        jnp.where(eye, near1[3 + r, REACH].astype(jnp.float32), 0.0) for r in range(2)
    )
    diagonals[0:1, :] = jnp.sum(on_diagonal, axis=0, keepdims=True)

    squares(near1, copies1)
    total_diagonal = jnp.zeros((1, BLK), jnp.float32)
    for r in range(2):
        mine = slice(r * BLK, (r + 1) * BLK)
        cubes = sum(
            square[mine, span(r + REACH + slot, 1)].astype(jnp.float32) * near1[3 + r, slot].astype(jnp.float32)
            for slot in range(SLOTS)
        )
        kept = jnp.where(eye, square[mine, span(2 * REACH + r, 1)].astype(jnp.float32), 0.0)
        value = 3.0 * jnp.sum(kept, axis=1, keepdims=True) - 2.0 * jnp.sum(cubes, axis=1, keepdims=True)
        value = jnp.where(pattern[r, REACH] == 1, value, 0.0).astype(jnp.bfloat16).astype(jnp.float32)
        total_diagonal += jnp.sum(jnp.where(eye, value, 0.0), axis=0, keepdims=True)
    diagonals[1:2, :] = total_diagonal

    def sum_copies(phase):
        size, me, partner, sums, arrived, first = phase
        sums[me] = diagonals[...]
        started = []
        for step in range(1, size):
            copy = pltpu.make_async_remote_copy(
                src_ref=diagonals,
                dst_ref=sums.at[me],
                send_sem=sum_send.at[first + step],
                recv_sem=arrived.at[me],
                device_id=partner(step),
                device_id_type=MESH,
            )
            copy.start()
            started.append(copy)
        return started

    def sum_wait(phase, started):
        size, me, _, sums, arrived, first = phase
        for step in range(1, size):
            other = lax.rem(me + step, size)
            pltpu.make_async_remote_copy(
                src_ref=diagonals,
                dst_ref=sums.at[other],
                send_sem=sum_send.at[first + step],
                recv_sem=arrived.at[other],
                device_id=phase[2](step),
                device_id_type=MESH,
            ).wait_recv()
        for copy in started:
            copy.wait_send()
        return functools.reduce(jnp.add, [sums[i] for i in range(size)])

    def finish(r, slot, value):
        last[r, slot] = value

    started = sum_copies(phases[0])
    update(near1, 0, finish)
    update(near1, 1, finish)
    diagonals[...] = sum_wait(phases[0], started)
    started = sum_copies(phases[1])
    update(near1, 2, finish)
    update(near1, 3, finish)
    store = pltpu.make_async_copy(last, purified, store_sem)
    store.start()
    diagonals[...] = sum_wait(phases[1], started)
    started = sum_copies(phases[2])
    for copy in copies0 + copies1:
        copy.wait_send()
    sums = sum_wait(phases[2], started)
    order = 2.0 * BLK * count
    for section in range(STEPS):
        occupation[section] = jnp.sum(sums[section : section + 1, :]) / order
    store.wait()


def on_device(sizes, pattern, density):
    rows, columns, inners = sizes
    chips, layers = CORES * inners, columns // CORES
    flat = pltpu.VMEM((WINDOW, SLOTS, BLK, BLK), jnp.bfloat16)
    wide = COLUMNS * BLK
    purified, occupation = pl.pallas_call(
        functools.partial(kernel, sizes),
        out_shape=(
            jax.ShapeDtypeStruct(density.shape, jnp.bfloat16),
            jax.ShapeDtypeStruct((STEPS,), jnp.float32),
        ),
        in_specs=[pl.BlockSpec(memory_space=pltpu.SMEM), pl.BlockSpec(memory_space=pl.ANY)],
        out_specs=(pl.BlockSpec(memory_space=pl.ANY), pl.BlockSpec(memory_space=pltpu.SMEM)),
        scratch_shapes=[
            flat,
            flat,
            pltpu.VMEM((2 * BLK, WINDOW * BLK), jnp.bfloat16),
            pltpu.VMEM((2 * BLK, wide), jnp.float32),
            pltpu.VMEM((2 * BLK, wide), jnp.bfloat16),
            pltpu.VMEM((2, SLOTS, BLK, BLK), jnp.bfloat16),
            pltpu.VMEM((STEPS, BLK), jnp.float32),
            pltpu.VMEM((chips, STEPS, BLK), jnp.float32),
            pltpu.VMEM((layers, STEPS, BLK), jnp.float32),
            pltpu.VMEM((rows, STEPS, BLK), jnp.float32),
            pltpu.SemaphoreType.DMA((STEPS, len(MESSAGES))),
            pltpu.SemaphoreType.DMA((STEPS, len(MESSAGES))),
            pltpu.SemaphoreType.DMA,
            pltpu.SemaphoreType.DMA,
            pltpu.SemaphoreType.DMA((chips + layers + rows,)),
            pltpu.SemaphoreType.DMA((chips,)),
            pltpu.SemaphoreType.DMA((layers,)),
            pltpu.SemaphoreType.DMA((rows,)),
        ],
        compiler_params=pltpu.CompilerParams(
            collective_id=0, has_side_effects=True, vmem_limit_bytes=40 * 2**20
        ),
        name="purify",
    )(pattern, density)
    return purified, occupation


def solution(mesh):
    sizes = tuple(mesh.shape[axis] for axis in ("row", "col", "inner"))
    return jax.shard_map(
        functools.partial(on_device, sizes),
        mesh=mesh,
        in_specs=(P(("row", "col", "inner"), None), P(("row", "col", "inner"), None, None, None)),
        out_specs=(P(("row", "col", "inner"), None, None, None), P()),
        check_vma=False,
    )
```

```python
import functools

import jax
import jax.numpy as jnp
from jax import lax
from jax.experimental import pallas as pl
from jax.experimental.pallas import tpu as pltpu
from jax.sharding import PartitionSpec as P

BLK = 128
REACH = 3
SLOTS = 7
STEPS = 2
CORES = 2
MESH = pl.DeviceIdType.MESH

WINDOW = 8
COLUMNS = WINDOW + SLOTS - 1

MESSAGES = (
    (4, 0, 4, 2, 1, None),
    (3, 3, 4, 5, -1, None),
    (3, 0, 4, 1, 1, None),
    (4, 3, 4, 6, -1, None),
    (2, 0, 4, 0, 1, 0),
    (5, 3, 4, 7, -1, 1),
    (4, 6, 1, 2, 1, None),
)
FROM_OWN = ((0, 6), (1, 5), (1, 6), (2, 4), (2, 5), (5, 1), (5, 2), (6, 0), (6, 1), (7, 0))
FROM_MESSAGE = {0: ((0, 5), (1, 4)), 1: ((6, 2), (7, 1)), 2: ((0, 4),), 3: ((7, 2),), 6: ((5, 0),)}


def wrapped(index, size):
    return jnp.where(index >= size, index - size, index)


def kernel(
    sizes, pattern_in, density, purified, occupation, near0, near1, left, total, square, cross, pattern,
    bit_out, bit_in, diagonals, sums_a, sums_b, sums_c, send_sem, recv_sem, bit_sem, load_sem,
    sum_send, recv_a, recv_b, recv_c,
):
    rows, columns, inners = sizes
    count = rows * columns * inners
    layers = columns // CORES
    row, col, inner = lax.axis_index("row"), lax.axis_index("col"), lax.axis_index("inner")
    layer, core = lax.div(col, CORES), lax.rem(col, CORES)

    load = pltpu.make_async_copy(density, near0.at[pl.ds(3, 2)], load_sem.at[0])
    load.start()
    load_pattern = pltpu.make_async_copy(pattern_in, pattern, load_sem.at[1])
    load_pattern.start()

    after_col = jnp.where(inner == inners - 1, col + 1, col)
    before_col = jnp.where(inner == 0, col - 1, col)
    after = (
        wrapped(jnp.where(after_col == columns, row + 1, row), rows),
        wrapped(after_col, columns),
        wrapped(inner + 1, inners),
    )
    before = (
        wrapped(jnp.where(before_col < 0, row - 1, row) + rows, rows),
        wrapped(before_col + columns, columns),
        wrapped(inner + inners - 1, inners),
    )
    near_place = {1: after, -1: before}

    def chip(core_, inner_):
        return core_ * inners + inner_

    group_a = []
    for core_step in range(CORES):
        for step in range(inners):
            if core_step or step:
                core_ = wrapped(core + core_step, CORES)
                inner_ = wrapped(inner + step, inners)
                group_a.append(((row, layer * CORES + core_, inner_), chip(core_, inner_)))
    group_b = [
        ((row, wrapped(layer + step, layers) * CORES + core, inner), wrapped(layer + step, layers))
        for step in range(1, layers)
    ]
    order = sorted(range(1, rows), key=lambda step: -min(step, rows - step))
    group_c = [((wrapped(row + step, rows), col, inner), wrapped(row + step, rows)) for step in order]
    phase_a = (CORES * inners, chip(core, inner), group_a, sums_a, recv_a, 0)
    phase_b = (layers, layer, group_b, sums_b, recv_b, CORES * inners)
    phase_c = (rows, row, group_c, sums_c, recv_c, CORES * inners + layers)

    barrier = pltpu.get_barrier_semaphore()
    greeted = 0
    for place in (after, before):
        pl.semaphore_signal(barrier, inc=1, device_id=place, device_id_type=MESH)
        greeted += 1
    for _, _, group, _, _, _ in (phase_a, phase_c, phase_b):
        for place, _ in group:
            pl.semaphore_signal(barrier, inc=1, device_id=place, device_id_type=MESH)
            greeted += 1
    zero_block = jnp.zeros((BLK, BLK), jnp.bfloat16)
    left[0:BLK, 7 * BLK : 8 * BLK] = zero_block
    left[BLK : 2 * BLK, 0:BLK] = zero_block
    left[2 * BLK : 3 * BLK, 6 * BLK : 7 * BLK] = zero_block
    left[2 * BLK : 3 * BLK, 7 * BLK : 8 * BLK] = zero_block
    load_pattern.wait()
    bit_out[...] = jnp.full((8, BLK), jnp.where(pattern[1, 2 * REACH] == 1, 1.0, 0.0), jnp.float32)
    load.wait()
    pl.semaphore_wait(barrier, greeted)

    eye = lax.broadcasted_iota(jnp.int32, (BLK, BLK), 0) == lax.broadcasted_iota(jnp.int32, (BLK, BLK), 1)

    def block(near, r, column):
        slot = column - r
        return near[r, slot] if 0 <= slot < SLOTS else zero_block

    def tile(near, r, column, width):
        return jnp.concatenate(
            [
                jnp.concatenate([block(near, r + i, column + j) for j in range(width)], axis=1)
                for i in range(2)
            ],
            axis=0,
        )

    def mirror(near, places):
        for r, slot in places:
            near[r, slot] = near[r + slot - REACH, 2 * REACH - slot].T

    def span(column, width=2):
        return slice(column * BLK, (column + width) * BLK)

    def across(a, b):
        return lax.dot_general(a, b, (((1,), (1,)), ((), ())), preferred_element_type=jnp.float32)

    def update(near, q, store):
        cube = across(square[0 : 2 * BLK, span(2 * q, 8)], tile(near, 2 * q, 2 * q, 8))
        for r in range(2):
            for j in range(2):
                slot = 2 * q + j - r
                if 0 <= slot < SLOTS:
                    mine = span(r, 1)
                    value = (
                        3.0 * square[mine, span(2 * q + j + REACH, 1)].astype(jnp.float32)
                        - 2.0 * cube[mine, span(j, 1)]
                    )
                    store(r, slot, jnp.where(pattern[r, slot] == 1, value, 0.0).astype(jnp.bfloat16))

    def exchange(section, near):
        copies = []
        for index, (r, slot, slots, target, direction, after) in enumerate(MESSAGES):
            if section and index == 6:
                continue
            copies.append(
                pltpu.make_async_remote_copy(
                    src_ref=near.at[r, pl.ds(slot, slots)],
                    dst_ref=near.at[target, pl.ds(slot, slots)],
                    send_sem=send_sem.at[section, index],
                    recv_sem=recv_sem.at[section, index],
                    device_id=near_place[direction],
                    device_id_type=MESH,
                )
            )
            if after is None:
                copies[-1].start()
        return copies

    def fill_left(near):
        for r in range(2):
            for slot in range(SLOTS):
                left[span(r, 1), span(slot + r, 1)] = near[3 + r, slot]

    def relay(copies):
        copies[0].wait_recv()
        copies[4].start()
        copies[1].wait_recv()
        copies[5].start()

    def height(section, column):
        return 3 * BLK if section == 0 and 4 <= column < 12 else 2 * BLK

    def first_half(section, near):
        mirror(near, FROM_MESSAGE[0])
        mirror(near, FROM_MESSAGE[1])
        if section == 0:
            for slot in range(1, SLOTS):
                left[span(2, 1), span(slot - 1, 1)] = near[2, slot]
        for column in range(2, 12, 2):
            high = height(section, column)
            terms = [
                jnp.dot(left[0:high, span(r)], tile(near, r, column, 2), preferred_element_type=jnp.float32)
                for r in (2, 4)
                if r - 1 <= column <= r + 7
            ]
            total[0:high, span(column)] = functools.reduce(jnp.add, terms)

    def second_half(section, near, copies):
        copies[2].wait_recv()
        copies[3].wait_recv()
        mirror(near, FROM_MESSAGE[2])
        mirror(near, FROM_MESSAGE[3])
        copies[4].wait_recv()
        copies[5].wait_recv()
        for column in range(0, COLUMNS, 2):
            high = height(section, column)
            terms = [total[0:high, span(column)]] if 2 <= column < 12 else []
            terms += [
                jnp.dot(left[0:high, span(r)], tile(near, r, column, 2), preferred_element_type=jnp.float32)
                for r in (0, 6)
                if r - 1 <= column <= r + 7
            ]
            value = functools.reduce(jnp.add, terms)
            if section == 0 and column == 4:
                extra = across(near[2, 0], near[2, 0])
                total[span(2, 1), span(5, 1)] = value[2 * BLK : 3 * BLK, BLK : 2 * BLK] + extra
            elif high == 3 * BLK:
                total[span(2, 1), span(column)] = value[2 * BLK : 3 * BLK]
            square[:, span(column)] = value[0 : 2 * BLK].astype(jnp.bfloat16)
        if section == 0:
            cross[...] = total[span(2, 1), span(5, 7)].astype(jnp.bfloat16)

    def send_sums(phase):
        size, me, group, sums, arrived, first = phase
        sums[me] = diagonals[...]
        started = []
        for index, (place, _) in enumerate(group):
            copy = pltpu.make_async_remote_copy(
                src_ref=diagonals,
                dst_ref=sums.at[me],
                send_sem=sum_send.at[first + index],
                recv_sem=arrived.at[me],
                device_id=place,
                device_id_type=MESH,
            )
            copy.start()
            started.append(copy)
        return started

    def receive_sums(phase, started):
        size, _, group, sums, arrived, first = phase
        for index, (place, other) in enumerate(group):
            pltpu.make_async_remote_copy(
                src_ref=diagonals,
                dst_ref=sums.at[other],
                send_sem=sum_send.at[first + index],
                recv_sem=arrived.at[other],
                device_id=place,
                device_id_type=MESH,
            ).wait_recv()
        for copy in started:
            copy.wait_send()
        return functools.reduce(jnp.add, [sums[i] for i in range(size)])

    def down(value):
        return jnp.sum(value, axis=0, keepdims=True)

    copies0 = exchange(0, near0)
    bit = pltpu.make_async_remote_copy(
        src_ref=bit_out,
        dst_ref=bit_in,
        send_sem=bit_sem.at[0],
        recv_sem=bit_sem.at[1],
        device_id=after,
        device_id_type=MESH,
    )
    bit.start()
    fill_left(near0)
    mirror(near0, FROM_OWN)
    relay(copies0)
    copies0[6].wait_recv()
    mirror(near0, FROM_MESSAGE[6])
    first_half(0, near0)
    second_half(0, near0, copies0)

    def keep(r, slot, value):
        near1[3 + r, slot] = value

    for q in range(4):
        update(near0, q, keep)
    copies1 = exchange(1, near1)
    bit.wait_recv()
    value = 3.0 * cross[:, span(3, 1)].astype(jnp.float32) - 2.0 * across(
        cross[...], jnp.concatenate([near0[5, slot] for slot in range(SLOTS)], axis=1)
    )
    near1[2, 6] = jnp.where(bit_in[0:1, :] == 1.0, value, 0.0).astype(jnp.bfloat16)
    fill_left(near1)

    diagonals[0:1, :] = down(
        sum(jnp.where(eye, near1[3 + r, REACH].astype(jnp.float32), 0.0) for r in range(2))
    )
    squares = sum(near1[3 + r, slot].astype(jnp.float32) ** 2 for r in range(2) for slot in range(SLOTS))
    own = left[0 : 2 * BLK, span(3)]
    outer = jnp.concatenate([left[0 : 2 * BLK, span(0, 3)], left[0 : 2 * BLK, span(5, 3)]], axis=1)
    gram = across(own, own) + 3.0 * across(outer, outer)
    cubes = own.astype(jnp.float32) * gram
    cubes = cubes[:, 0:BLK] + cubes[:, BLK : 2 * BLK]
    far = jnp.dot(left[0 : 2 * BLK, span(2, 1)], near1[2, 6], preferred_element_type=jnp.float32)
    cubes += 6.0 * far * left[0 : 2 * BLK, span(5, 1)].astype(jnp.float32)
    diagonals[1:2, :] = 3.0 * down(squares) - 2.0 * down(cubes)

    started = send_sums(phase_a)
    mirror(near1, FROM_OWN)
    mirror(near1, FROM_MESSAGE[6])
    diagonals[...] = receive_sums(phase_a, started)
    started = send_sums(phase_c)
    relay(copies1)
    first_half(1, near1)
    diagonals[...] = receive_sums(phase_c, started)
    started = send_sums(phase_b)
    second_half(1, near1, copies1)

    def finish(r, slot, value):
        purified[r, slot] = value

    for q in range(4):
        update(near1, q, finish)
    for copy in copies0 + copies1:
        copy.wait_send()
    bit.wait_send()
    occupation[...] = receive_sums(phase_b, started)


def on_device(sizes, pattern, density):
    rows, columns, inners = sizes
    chips, layers = CORES * inners, columns // CORES
    flat = pltpu.VMEM((WINDOW, SLOTS, BLK, BLK), jnp.bfloat16)
    wide = COLUMNS * BLK
    purified, sums = pl.pallas_call(
        functools.partial(kernel, sizes),
        out_shape=(
            pltpu.VMEM(density.shape, jnp.bfloat16),
            pltpu.VMEM((STEPS, BLK), jnp.float32),
        ),
        in_specs=[pl.BlockSpec(memory_space=pltpu.HBM), pl.BlockSpec(memory_space=pltpu.HBM)],
        out_specs=(pl.BlockSpec(memory_space=pltpu.VMEM), pl.BlockSpec(memory_space=pltpu.VMEM)),
        scratch_shapes=[
            flat,
            flat,
            pltpu.VMEM((3 * BLK, WINDOW * BLK), jnp.bfloat16),
            pltpu.VMEM((3 * BLK, wide), jnp.float32),
            pltpu.VMEM((2 * BLK, wide), jnp.bfloat16),
            pltpu.VMEM((BLK, SLOTS * BLK), jnp.bfloat16),
            pltpu.SMEM((2, SLOTS), jnp.int32),
            pltpu.VMEM((8, BLK), jnp.float32),
            pltpu.VMEM((8, BLK), jnp.float32),
            pltpu.VMEM((STEPS, BLK), jnp.float32),
            pltpu.VMEM((chips, STEPS, BLK), jnp.float32),
            pltpu.VMEM((layers, STEPS, BLK), jnp.float32),
            pltpu.VMEM((rows, STEPS, BLK), jnp.float32),
            pltpu.SemaphoreType.DMA((STEPS, len(MESSAGES))),
            pltpu.SemaphoreType.DMA((STEPS, len(MESSAGES))),
            pltpu.SemaphoreType.DMA((2,)),
            pltpu.SemaphoreType.DMA((2,)),
            pltpu.SemaphoreType.DMA((chips + layers + rows,)),
            pltpu.SemaphoreType.DMA((chips,)),
            pltpu.SemaphoreType.DMA((layers,)),
            pltpu.SemaphoreType.DMA((rows,)),
        ],
        compiler_params=pltpu.CompilerParams(
            collective_id=0, has_side_effects=True, vmem_limit_bytes=56 * 2**20
        ),
        name="purify",
    )(pattern, density)
    order = 2.0 * BLK * rows * columns * inners
    return purified, jnp.sum(sums, axis=1) / order


def solution(mesh):
    sizes = tuple(mesh.shape[axis] for axis in ("row", "col", "inner"))
    return jax.shard_map(
        functools.partial(on_device, sizes),
        mesh=mesh,
        in_specs=(P(("row", "col", "inner"), None), P(("row", "col", "inner"), None, None, None)),
        out_specs=(P(("row", "col", "inner"), None, None, None), P()),
        check_vma=False,
    )
```

```python
import functools

import jax
import jax.numpy as jnp
from jax import lax
from jax.experimental import pallas as pl
from jax.experimental.pallas import tpu as pltpu
from jax.sharding import PartitionSpec as P

BLK = 128
REACH = 3
SLOTS = 7
STEPS = 2
CORES = 2
MESH = pl.DeviceIdType.MESH

WINDOW = 8
COLUMNS = WINDOW + SLOTS - 1

MESSAGES = (
    (4, 0, 4, 2, 1, None),
    (3, 3, 4, 5, -1, None),
    (3, 0, 4, 1, 1, None),
    (4, 3, 4, 6, -1, None),
    (2, 0, 4, 0, 1, 0),
    (5, 3, 4, 7, -1, 1),
    (4, 6, 1, 2, 1, None),
)
FROM_OWN = ((0, 6), (1, 5), (1, 6), (2, 4), (2, 5), (5, 1), (5, 2), (6, 0), (6, 1), (7, 0))
FROM_MESSAGE = {0: ((0, 5), (1, 4)), 1: ((6, 2), (7, 1)), 2: ((0, 4),), 3: ((7, 2),), 6: ((5, 0),)}


def wrapped(index, size):
    return jnp.where(index >= size, index - size, index)


def kernel(
    sizes, pattern_in, density, purified, occupation, near0, near1, left, total, square, cross, pattern,
    bit_out, bit_in, sums_a, sums_b, sums_c, send_sem, recv_sem, bit_sem, load_sem,
    sum_send, recv_a, recv_b, recv_c,
):
    rows, columns, inners = sizes
    count = rows * columns * inners
    layers = columns // CORES
    row, col, inner = lax.axis_index("row"), lax.axis_index("col"), lax.axis_index("inner")
    layer, core = lax.div(col, CORES), lax.rem(col, CORES)

    load = pltpu.make_async_copy(density, near0.at[pl.ds(3, 2)], load_sem.at[0])
    load.start()
    load_pattern = pltpu.make_async_copy(pattern_in, pattern, load_sem.at[1])
    load_pattern.start()

    after_col = jnp.where(inner == inners - 1, col + 1, col)
    before_col = jnp.where(inner == 0, col - 1, col)
    after = (
        wrapped(jnp.where(after_col == columns, row + 1, row), rows),
        wrapped(after_col, columns),
        wrapped(inner + 1, inners),
    )
    before = (
        wrapped(jnp.where(before_col < 0, row - 1, row) + rows, rows),
        wrapped(before_col + columns, columns),
        wrapped(inner + inners - 1, inners),
    )
    near_place = {1: after, -1: before}

    def chip(core_, inner_):
        return core_ * inners + inner_

    group_a = []
    for core_step in range(CORES):
        for step in range(inners):
            if core_step or step:
                core_ = wrapped(core + core_step, CORES)
                inner_ = wrapped(inner + step, inners)
                group_a.append(((row, layer * CORES + core_, inner_), chip(core_, inner_)))
    group_b = [
        ((row, wrapped(layer + step, layers) * CORES + core, inner), wrapped(layer + step, layers))
        for step in range(1, layers)
    ]
    order = sorted(range(1, rows), key=lambda step: -min(step, rows - step))
    group_c = [((wrapped(row + step, rows), col, inner), wrapped(row + step, rows)) for step in order]
    phase_a = (CORES * inners, chip(core, inner), group_a, sums_a, recv_a, 0)
    phase_b = (layers, layer, group_b, sums_b, recv_b, CORES * inners)
    phase_c = (rows, row, group_c, sums_c, recv_c, CORES * inners + layers)

    barrier = pltpu.get_barrier_semaphore()
    greeted = 0
    for place in (after, before):
        pl.semaphore_signal(barrier, inc=1, device_id=place, device_id_type=MESH)
        greeted += 1
    for _, _, group, _, _, _ in (phase_a, phase_c, phase_b):
        for place, _ in group:
            pl.semaphore_signal(barrier, inc=1, device_id=place, device_id_type=MESH)
            greeted += 1
    zero_block = jnp.zeros((BLK, BLK), jnp.bfloat16)
    left[0:BLK, 7 * BLK : 8 * BLK] = zero_block
    left[BLK : 2 * BLK, 0:BLK] = zero_block
    left[2 * BLK : 3 * BLK, 6 * BLK : 7 * BLK] = zero_block
    left[2 * BLK : 3 * BLK, 7 * BLK : 8 * BLK] = zero_block
    load_pattern.wait()
    bit_out[...] = jnp.full((8, BLK), jnp.where(pattern[1, 2 * REACH] == 1, 1.0, 0.0), jnp.float32)
    pl.semaphore_wait(barrier, greeted)

    eye = lax.broadcasted_iota(jnp.int32, (BLK, BLK), 0) == lax.broadcasted_iota(jnp.int32, (BLK, BLK), 1)

    def block(near, r, column):
        slot = column - r
        return near[r, slot] if 0 <= slot < SLOTS else zero_block

    def tile(near, r, column, width):
        return jnp.concatenate(
            [
                jnp.concatenate([block(near, r + i, column + j) for j in range(width)], axis=1)
                for i in range(2)
            ],
            axis=0,
        )

    def mirror(near, places):
        for r, slot in places:
            near[r, slot] = near[r + slot - REACH, 2 * REACH - slot].T

    def span(column, width=2):
        return slice(column * BLK, (column + width) * BLK)

    def across(a, b):
        return lax.dot_general(a, b, (((1,), (1,)), ((), ())), preferred_element_type=jnp.float32)

    def update(near, q, store):
        cube = across(square[0 : 2 * BLK, span(2 * q, 8)], tile(near, 2 * q, 2 * q, 8))
        for r in range(2):
            for j in range(2):
                slot = 2 * q + j - r
                if 0 <= slot < SLOTS:
                    mine = span(r, 1)
                    value = (
                        3.0 * square[mine, span(2 * q + j + REACH, 1)].astype(jnp.float32)
                        - 2.0 * cube[mine, span(j, 1)]
                    )
                    store(r, slot, jnp.where(pattern[r, slot] == 1, value, 0.0).astype(jnp.bfloat16))

    def exchange(section, near):
        copies = []
        for index, (r, slot, slots, target, direction, after) in enumerate(MESSAGES):
            if section and index == 6:
                continue
            copies.append(
                pltpu.make_async_remote_copy(
                    src_ref=density.at[r - 3, pl.ds(slot, slots)]
                    if section == 0 and after is None
                    else near.at[r, pl.ds(slot, slots)],
                    dst_ref=near.at[target, pl.ds(slot, slots)],
                    send_sem=send_sem.at[section, index],
                    recv_sem=recv_sem.at[section, index],
                    device_id=near_place[direction],
                    device_id_type=MESH,
                )
            )
            if after is None:
                copies[-1].start()
        return copies

    def fill_left(near):
        for r in range(2):
            for slot in range(SLOTS):
                left[span(r, 1), span(slot + r, 1)] = near[3 + r, slot]

    def relay(copies):
        copies[0].wait_recv()
        copies[4].start()
        copies[1].wait_recv()
        copies[5].start()

    def height(section, column):
        return 3 * BLK if section == 0 and 4 <= column < 12 else 2 * BLK

    def first_half(section, near):
        mirror(near, FROM_MESSAGE[0])
        mirror(near, FROM_MESSAGE[1])
        if section == 0:
            for slot in range(1, SLOTS):
                left[span(2, 1), span(slot - 1, 1)] = near[2, slot]
        for column in range(2, 12, 2):
            high = height(section, column)
            terms = [
                jnp.dot(left[0:high, span(r)], tile(near, r, column, 2), preferred_element_type=jnp.float32)
                for r in (2, 4)
                if r - 1 <= column <= r + 7
            ]
            total[0:high, span(column)] = functools.reduce(jnp.add, terms)

    def second_half(section, near, copies):
        copies[2].wait_recv()
        copies[3].wait_recv()
        mirror(near, FROM_MESSAGE[2])
        mirror(near, FROM_MESSAGE[3])
        copies[4].wait_recv()
        copies[5].wait_recv()
        for column in range(0, COLUMNS, 2):
            high = height(section, column)
            terms = [total[0:high, span(column)]] if 2 <= column < 12 else []
            terms += [
                jnp.dot(left[0:high, span(r)], tile(near, r, column, 2), preferred_element_type=jnp.float32)
                for r in (0, 6)
                if r - 1 <= column <= r + 7
            ]
            value = functools.reduce(jnp.add, terms)
            if section == 0 and column == 4:
                extra = across(near[2, 0], near[2, 0])
                total[span(2, 1), span(5, 1)] = value[2 * BLK : 3 * BLK, BLK : 2 * BLK] + extra
            elif high == 3 * BLK:
                total[span(2, 1), span(column)] = value[2 * BLK : 3 * BLK]
            square[:, span(column)] = value[0 : 2 * BLK].astype(jnp.bfloat16)
        if section == 0:
            cross[...] = total[span(2, 1), span(5, 7)].astype(jnp.bfloat16)

    def send_sums(phase):
        size, me, group, sums, arrived, first = phase
        started = []
        for index, (place, _) in enumerate(group):
            copy = pltpu.make_async_remote_copy(
                src_ref=sums.at[me],
                dst_ref=sums.at[me],
                send_sem=sum_send.at[first + index],
                recv_sem=arrived.at[me],
                device_id=place,
                device_id_type=MESH,
            )
            copy.start()
            started.append(copy)
        return started

    def receive_sums(phase):
        size, me, group, sums, arrived, first = phase
        for index, (place, other) in enumerate(group):
            pltpu.make_async_remote_copy(
                src_ref=sums.at[me],
                dst_ref=sums.at[other],
                send_sem=sum_send.at[first + index],
                recv_sem=arrived.at[other],
                device_id=place,
                device_id_type=MESH,
            ).wait_recv()
        return functools.reduce(jnp.add, [sums[i] for i in range(size)])

    def down(value):
        return jnp.sum(value, axis=0, keepdims=True)

    copies0 = exchange(0, near0)
    bit = pltpu.make_async_remote_copy(
        src_ref=bit_out,
        dst_ref=bit_in,
        send_sem=bit_sem.at[0],
        recv_sem=bit_sem.at[1],
        device_id=after,
        device_id_type=MESH,
    )
    bit.start()
    load.wait()
    fill_left(near0)
    mirror(near0, FROM_OWN)
    relay(copies0)
    copies0[6].wait_recv()
    mirror(near0, FROM_MESSAGE[6])
    first_half(0, near0)
    second_half(0, near0, copies0)

    def keep(r, slot, value):
        near1[3 + r, slot] = value

    for q in range(4):
        update(near0, q, keep)
    bit.wait_recv()
    value = 3.0 * cross[:, span(3, 1)].astype(jnp.float32) - 2.0 * across(
        cross[...], jnp.concatenate([near0[5, slot] for slot in range(SLOTS)], axis=1)
    )
    near1[2, 6] = jnp.where(bit_in[0:1, :] == 1.0, value, 0.0).astype(jnp.bfloat16)
    fill_left(near1)

    sums_a[phase_a[1], 0:1] = down(
        sum(jnp.where(eye, near1[3 + r, REACH].astype(jnp.float32), 0.0) for r in range(2))
    )
    squares = sum(near1[3 + r, slot].astype(jnp.float32) ** 2 for r in range(2) for slot in range(SLOTS))
    own = left[0 : 2 * BLK, span(3)]
    outer = jnp.concatenate([left[0 : 2 * BLK, span(0, 3)], left[0 : 2 * BLK, span(5, 3)]], axis=1)
    gram = across(own, own) + 3.0 * across(outer, outer)
    cubes = own.astype(jnp.float32) * gram
    cubes = cubes[:, 0:BLK] + cubes[:, BLK : 2 * BLK]
    far = jnp.dot(left[0 : 2 * BLK, span(2, 1)], near1[2, 6], preferred_element_type=jnp.float32)
    cubes += 6.0 * far * left[0 : 2 * BLK, span(5, 1)].astype(jnp.float32)
    sums_a[phase_a[1], 1:2] = 3.0 * down(squares) - 2.0 * down(cubes)

    sent = send_sums(phase_a)
    copies1 = exchange(1, near1)
    mirror(near1, FROM_OWN)
    mirror(near1, FROM_MESSAGE[6])
    sums_c[phase_c[1]] = receive_sums(phase_a)
    sent += send_sums(phase_c)
    relay(copies1)
    first_half(1, near1)
    sums_b[phase_b[1]] = receive_sums(phase_c)
    sent += send_sums(phase_b)
    second_half(1, near1, copies1)

    def finish(r, slot, value):
        purified[r, slot] = value

    for q in range(4):
        update(near1, q, finish)
    for copy in copies0 + copies1 + [bit] + sent[: len(group_a) + len(group_c)]:
        copy.wait_send()
    occupation[...] = receive_sums(phase_b)
    for copy in sent[len(group_a) + len(group_c) :]:
        copy.wait_send()


def on_device(sizes, pattern, density):
    rows, columns, inners = sizes
    chips, layers = CORES * inners, columns // CORES
    flat = pltpu.VMEM((WINDOW, SLOTS, BLK, BLK), jnp.bfloat16)
    wide = COLUMNS * BLK
    purified, sums = pl.pallas_call(
        functools.partial(kernel, sizes),
        out_shape=(
            pltpu.VMEM(density.shape, jnp.bfloat16),
            pltpu.VMEM((STEPS, BLK), jnp.float32),
        ),
        in_specs=[pl.BlockSpec(memory_space=pltpu.HBM), pl.BlockSpec(memory_space=pltpu.HBM)],
        out_specs=(pl.BlockSpec(memory_space=pltpu.VMEM), pl.BlockSpec(memory_space=pltpu.VMEM)),
        scratch_shapes=[
            flat,
            flat,
            pltpu.VMEM((3 * BLK, WINDOW * BLK), jnp.bfloat16),
            pltpu.VMEM((3 * BLK, wide), jnp.float32),
            pltpu.VMEM((2 * BLK, wide), jnp.bfloat16),
            pltpu.VMEM((BLK, SLOTS * BLK), jnp.bfloat16),
            pltpu.SMEM((2, SLOTS), jnp.int32),
            pltpu.VMEM((8, BLK), jnp.float32),
            pltpu.VMEM((8, BLK), jnp.float32),
            pltpu.VMEM((chips, STEPS, BLK), jnp.float32),
            pltpu.VMEM((layers, STEPS, BLK), jnp.float32),
            pltpu.VMEM((rows, STEPS, BLK), jnp.float32),
            pltpu.SemaphoreType.DMA((STEPS, len(MESSAGES))),
            pltpu.SemaphoreType.DMA((STEPS, len(MESSAGES))),
            pltpu.SemaphoreType.DMA((2,)),
            pltpu.SemaphoreType.DMA((2,)),
            pltpu.SemaphoreType.DMA((chips + layers + rows,)),
            pltpu.SemaphoreType.DMA((chips,)),
            pltpu.SemaphoreType.DMA((layers,)),
            pltpu.SemaphoreType.DMA((rows,)),
        ],
        compiler_params=pltpu.CompilerParams(
            collective_id=0, has_side_effects=True, vmem_limit_bytes=56 * 2**20
        ),
        name="purify",
    )(pattern, density)
    order = 2.0 * BLK * rows * columns * inners
    return purified, jnp.sum(sums, axis=1) / order


def solution(mesh):
    sizes = tuple(mesh.shape[axis] for axis in ("row", "col", "inner"))
    return jax.shard_map(
        functools.partial(on_device, sizes),
        mesh=mesh,
        in_specs=(P(("row", "col", "inner"), None), P(("row", "col", "inner"), None, None, None)),
        out_specs=(P(("row", "col", "inner"), None, None, None), P()),
        check_vma=False,
    )
```

```python
import functools

import jax
import jax.numpy as jnp
from jax import lax
from jax.experimental import pallas as pl
from jax.experimental.pallas import tpu as pltpu
from jax.sharding import PartitionSpec as P

BLK = 128
REACH = 3
SLOTS = 7
STEPS = 2
CORES = 2
MESH = pl.DeviceIdType.MESH

WINDOW = 8
COLUMNS = WINDOW + SLOTS - 1

MESSAGES = (
    (4, 0, 4, 2, 1, None),
    (3, 3, 4, 5, -1, None),
    (3, 0, 4, 1, 1, None),
    (4, 3, 4, 6, -1, None),
    (2, 0, 4, 0, 1, 0),
    (5, 3, 4, 7, -1, 1),
    (4, 6, 1, 2, 1, None),
)
FROM_OWN = ((0, 6), (1, 5), (1, 6), (2, 4), (2, 5), (5, 1), (5, 2), (6, 0), (6, 1), (7, 0))
FROM_MESSAGE = {0: ((0, 5), (1, 4)), 1: ((6, 2), (7, 1)), 2: ((0, 4),), 3: ((7, 2),), 6: ((5, 0),)}


def wrapped(index, size):
    return jnp.where(index >= size, index - size, index)


def kernel(
    sizes, pattern_in, density, purified, occupation, near0, near1, left, total, square, cross, pattern,
    bit_out, bit_in, sums_a, sums_b, sums_c, send_sem, recv_sem, bit_sem, load_sem,
    sum_send, recv_a, recv_b, recv_c, in_above, in_below,
):
    rows, columns, inners = sizes
    count = rows * columns * inners
    layers = columns // CORES
    row, col, inner = lax.axis_index("row"), lax.axis_index("col"), lax.axis_index("inner")
    layer, core = lax.div(col, CORES), lax.rem(col, CORES)

    load = pltpu.make_async_copy(density, near0.at[pl.ds(3, 2)], load_sem.at[0])
    load.start()
    load_pattern = pltpu.make_async_copy(pattern_in, pattern, load_sem.at[1])
    load_pattern.start()

    after_col = jnp.where(inner == inners - 1, col + 1, col)
    before_col = jnp.where(inner == 0, col - 1, col)
    after = (
        wrapped(jnp.where(after_col == columns, row + 1, row), rows),
        wrapped(after_col, columns),
        wrapped(inner + 1, inners),
    )
    before = (
        wrapped(jnp.where(before_col < 0, row - 1, row) + rows, rows),
        wrapped(before_col + columns, columns),
        wrapped(inner + inners - 1, inners),
    )
    near_place = {1: after, -1: before}

    def chip(core_, inner_):
        return core_ * inners + inner_

    group_a = []
    for core_step in range(CORES):
        for step in range(inners):
            if core_step or step:
                core_ = wrapped(core + core_step, CORES)
                inner_ = wrapped(inner + step, inners)
                group_a.append(((row, layer * CORES + core_, inner_), chip(core_, inner_)))
    group_b = [
        ((row, wrapped(layer + step, layers) * CORES + core, inner), wrapped(layer + step, layers))
        for step in range(1, layers)
    ]
    order = sorted(range(1, rows), key=lambda step: -min(step, rows - step))
    group_c = [((wrapped(row + step, rows), col, inner), wrapped(row + step, rows)) for step in order]
    phase_a = (CORES * inners, chip(core, inner), group_a, sums_a, recv_a, 0)
    phase_b = (layers, layer, group_b, sums_b, recv_b, CORES * inners)
    phase_c = (rows, row, group_c, sums_c, recv_c, CORES * inners + layers)

    barrier = pltpu.get_barrier_semaphore()
    greeted = 0
    for place in (after, before):
        pl.semaphore_signal(barrier, inc=1, device_id=place, device_id_type=MESH)
        greeted += 1
    lines = []
    for axis, (size, at) in enumerate(
        (
            (rows, lambda step: (wrapped(row + step, rows), col, inner)),
            (layers, lambda step: (row, wrapped(layer + step, layers) * CORES + core, inner)),
        )
    ):
        if size > 1:
            lines.append((axis, size, at(1), at(size - 1)))
    greetings = [place for place, _ in group_a]
    for _, size, above, below in lines:
        greetings += [above] if size == 2 else [above, below]
    for place in greetings:
        pl.semaphore_signal(barrier, inc=1, device_id=place, device_id_type=MESH)
        greeted += 1
    zero_block = jnp.zeros((BLK, BLK), jnp.bfloat16)
    left[0:BLK, 7 * BLK : 8 * BLK] = zero_block
    left[BLK : 2 * BLK, 0:BLK] = zero_block
    left[2 * BLK : 3 * BLK, 6 * BLK : 7 * BLK] = zero_block
    left[2 * BLK : 3 * BLK, 7 * BLK : 8 * BLK] = zero_block
    load_pattern.wait()
    bit_out[...] = jnp.full((8, BLK), jnp.where(pattern[1, 2 * REACH] == 1, 1.0, 0.0), jnp.float32)
    pl.semaphore_wait(barrier, greeted)

    def spread(turn):
        for axis, size, above, below in lines:
            if turn < size // 2 - 1:
                pl.semaphore_signal(in_above.at[axis, turn], inc=1, device_id=below, device_id_type=MESH)
            if turn < (size - 1) // 2 - 1:
                pl.semaphore_signal(in_below.at[axis, turn], inc=1, device_id=above, device_id_type=MESH)

    def learn(turn):
        for axis, size, above, below in lines:
            if turn < size // 2 - 1:
                pl.semaphore_wait(in_above.at[axis, turn], 1)
            if turn < (size - 1) // 2 - 1:
                pl.semaphore_wait(in_below.at[axis, turn], 1)

    turns = max([size // 2 - 1 for _, size, _, _ in lines] + [0])

    eye = lax.broadcasted_iota(jnp.int32, (BLK, BLK), 0) == lax.broadcasted_iota(jnp.int32, (BLK, BLK), 1)

    def block(near, r, column):
        slot = column - r
        return near[r, slot] if 0 <= slot < SLOTS else zero_block

    def tile(near, r, column, width):
        return jnp.concatenate(
            [
                jnp.concatenate([block(near, r + i, column + j) for j in range(width)], axis=1)
                for i in range(2)
            ],
            axis=0,
        )

    def mirror(near, places):
        for r, slot in places:
            near[r, slot] = near[r + slot - REACH, 2 * REACH - slot].T

    def span(column, width=2):
        return slice(column * BLK, (column + width) * BLK)

    def across(a, b):
        return lax.dot_general(a, b, (((1,), (1,)), ((), ())), preferred_element_type=jnp.float32)

    def update(near, q, store):
        cube = across(square[0 : 2 * BLK, span(2 * q, 8)], tile(near, 2 * q, 2 * q, 8))
        for r in range(2):
            for j in range(2):
                slot = 2 * q + j - r
                if 0 <= slot < SLOTS:
                    mine = span(r, 1)
                    value = (
                        3.0 * square[mine, span(2 * q + j + REACH, 1)].astype(jnp.float32)
                        - 2.0 * cube[mine, span(j, 1)]
                    )
                    store(r, slot, jnp.where(pattern[r, slot] == 1, value, 0.0).astype(jnp.bfloat16))

    def exchange(section, near):
        copies = []
        for index, (r, slot, slots, target, direction, after) in enumerate(MESSAGES):
            if section and index == 6:
                continue
            copies.append(
                pltpu.make_async_remote_copy(
                    src_ref=density.at[r - 3, pl.ds(slot, slots)]
                    if section == 0 and after is None
                    else near.at[r, pl.ds(slot, slots)],
                    dst_ref=near.at[target, pl.ds(slot, slots)],
                    send_sem=send_sem.at[section, index],
                    recv_sem=recv_sem.at[section, index],
                    device_id=near_place[direction],
                    device_id_type=MESH,
                )
            )
            if after is None:
                copies[-1].start()
        return copies

    def fill_left(near):
        for r in range(2):
            for slot in range(SLOTS):
                left[span(r, 1), span(slot + r, 1)] = near[3 + r, slot]

    def relay(copies):
        copies[0].wait_recv()
        copies[4].start()
        copies[1].wait_recv()
        copies[5].start()

    def height(section, column):
        return 3 * BLK if section == 0 and 4 <= column < 12 else 2 * BLK

    def first_half(section, near):
        mirror(near, FROM_MESSAGE[0])
        mirror(near, FROM_MESSAGE[1])
        if section == 0:
            for slot in range(1, SLOTS):
                left[span(2, 1), span(slot - 1, 1)] = near[2, slot]
        for column in range(2, 12, 2):
            high = height(section, column)
            terms = [
                jnp.dot(left[0:high, span(r)], tile(near, r, column, 2), preferred_element_type=jnp.float32)
                for r in (2, 4)
                if r - 1 <= column <= r + 7
            ]
            total[0:high, span(column)] = functools.reduce(jnp.add, terms)

    def second_half(section, near, copies):
        copies[2].wait_recv()
        copies[3].wait_recv()
        mirror(near, FROM_MESSAGE[2])
        mirror(near, FROM_MESSAGE[3])
        if section == 0:
            learn(3)
            spread(4)
        copies[4].wait_recv()
        copies[5].wait_recv()
        for column in range(0, COLUMNS, 2):
            high = height(section, column)
            terms = [total[0:high, span(column)]] if 2 <= column < 12 else []
            terms += [
                jnp.dot(left[0:high, span(r)], tile(near, r, column, 2), preferred_element_type=jnp.float32)
                for r in (0, 6)
                if r - 1 <= column <= r + 7
            ]
            value = functools.reduce(jnp.add, terms)
            if section == 0 and column == 4:
                extra = across(near[2, 0], near[2, 0])
                total[span(2, 1), span(5, 1)] = value[2 * BLK : 3 * BLK, BLK : 2 * BLK] + extra
            elif high == 3 * BLK:
                total[span(2, 1), span(column)] = value[2 * BLK : 3 * BLK]
            square[:, span(column)] = value[0 : 2 * BLK].astype(jnp.bfloat16)
        if section == 0:
            cross[...] = total[span(2, 1), span(5, 7)].astype(jnp.bfloat16)

    def send_sums(phase):
        size, me, group, sums, arrived, first = phase
        started = []
        for index, (place, _) in enumerate(group):
            copy = pltpu.make_async_remote_copy(
                src_ref=sums.at[me],
                dst_ref=sums.at[me],
                send_sem=sum_send.at[first + index],
                recv_sem=arrived.at[me],
                device_id=place,
                device_id_type=MESH,
            )
            copy.start()
            started.append(copy)
        return started

    def receive_sums(phase):
        size, me, group, sums, arrived, first = phase
        for index, (place, other) in enumerate(group):
            pltpu.make_async_remote_copy(
                src_ref=sums.at[me],
                dst_ref=sums.at[other],
                send_sem=sum_send.at[first + index],
                recv_sem=arrived.at[other],
                device_id=place,
                device_id_type=MESH,
            ).wait_recv()
        return functools.reduce(jnp.add, [sums[i] for i in range(size)])

    def down(value):
        return jnp.sum(value, axis=0, keepdims=True)

    copies0 = exchange(0, near0)
    bit = pltpu.make_async_remote_copy(
        src_ref=bit_out,
        dst_ref=bit_in,
        send_sem=bit_sem.at[0],
        recv_sem=bit_sem.at[1],
        device_id=after,
        device_id_type=MESH,
    )
    bit.start()
    spread(0)
    load.wait()
    fill_left(near0)
    mirror(near0, FROM_OWN)
    learn(0)
    spread(1)
    relay(copies0)
    learn(1)
    spread(2)
    copies0[6].wait_recv()
    mirror(near0, FROM_MESSAGE[6])
    first_half(0, near0)
    learn(2)
    spread(3)
    second_half(0, near0, copies0)

    def keep(r, slot, value):
        near1[3 + r, slot] = value

    for q in range(4):
        update(near0, q, keep)
    bit.wait_recv()
    value = 3.0 * cross[:, span(3, 1)].astype(jnp.float32) - 2.0 * across(
        cross[...], jnp.concatenate([near0[5, slot] for slot in range(SLOTS)], axis=1)
    )
    near1[2, 6] = jnp.where(bit_in[0:1, :] == 1.0, value, 0.0).astype(jnp.bfloat16)
    fill_left(near1)

    sums_a[phase_a[1], 0:1] = down(
        sum(jnp.where(eye, near1[3 + r, REACH].astype(jnp.float32), 0.0) for r in range(2))
    )
    squares = sum(near1[3 + r, slot].astype(jnp.float32) ** 2 for r in range(2) for slot in range(SLOTS))
    own = left[0 : 2 * BLK, span(3)]
    outer = jnp.concatenate([left[0 : 2 * BLK, span(0, 3)], left[0 : 2 * BLK, span(5, 3)]], axis=1)
    gram = across(own, own) + 3.0 * across(outer, outer)
    cubes = own.astype(jnp.float32) * gram
    cubes = cubes[:, 0:BLK] + cubes[:, BLK : 2 * BLK]
    far = jnp.dot(left[0 : 2 * BLK, span(2, 1)], near1[2, 6], preferred_element_type=jnp.float32)
    cubes += 6.0 * far * left[0 : 2 * BLK, span(5, 1)].astype(jnp.float32)
    sums_a[phase_a[1], 1:2] = 3.0 * down(squares) - 2.0 * down(cubes)

    sent = send_sums(phase_a)
    copies1 = exchange(1, near1)
    mirror(near1, FROM_OWN)
    mirror(near1, FROM_MESSAGE[6])
    sums_c[phase_c[1]] = receive_sums(phase_a)
    sent += send_sums(phase_c)
    relay(copies1)
    first_half(1, near1)
    sums_b[phase_b[1]] = receive_sums(phase_c)
    for turn in range(4, turns):
        learn(turn)
        spread(turn + 1)
    sent += send_sums(phase_b)
    second_half(1, near1, copies1)

    def finish(r, slot, value):
        purified[r, slot] = value

    for q in range(4):
        update(near1, q, finish)
    for copy in copies0 + copies1 + [bit] + sent[: len(group_a) + len(group_c)]:
        copy.wait_send()
    occupation[...] = receive_sums(phase_b)
    for copy in sent[len(group_a) + len(group_c) :]:
        copy.wait_send()


def on_device(sizes, pattern, density):
    rows, columns, inners = sizes
    chips, layers = CORES * inners, columns // CORES
    flat = pltpu.VMEM((WINDOW, SLOTS, BLK, BLK), jnp.bfloat16)
    wide = COLUMNS * BLK
    purified, sums = pl.pallas_call(
        functools.partial(kernel, sizes),
        out_shape=(
            pltpu.VMEM(density.shape, jnp.bfloat16),
            pltpu.VMEM((STEPS, BLK), jnp.float32),
        ),
        in_specs=[pl.BlockSpec(memory_space=pltpu.HBM), pl.BlockSpec(memory_space=pltpu.HBM)],
        out_specs=(pl.BlockSpec(memory_space=pltpu.VMEM), pl.BlockSpec(memory_space=pltpu.VMEM)),
        scratch_shapes=[
            flat,
            flat,
            pltpu.VMEM((3 * BLK, WINDOW * BLK), jnp.bfloat16),
            pltpu.VMEM((3 * BLK, wide), jnp.float32),
            pltpu.VMEM((2 * BLK, wide), jnp.bfloat16),
            pltpu.VMEM((BLK, SLOTS * BLK), jnp.bfloat16),
            pltpu.SMEM((2, SLOTS), jnp.int32),
            pltpu.VMEM((8, BLK), jnp.float32),
            pltpu.VMEM((8, BLK), jnp.float32),
            pltpu.VMEM((chips, STEPS, BLK), jnp.float32),
            pltpu.VMEM((layers, STEPS, BLK), jnp.float32),
            pltpu.VMEM((rows, STEPS, BLK), jnp.float32),
            pltpu.SemaphoreType.DMA((STEPS, len(MESSAGES))),
            pltpu.SemaphoreType.DMA((STEPS, len(MESSAGES))),
            pltpu.SemaphoreType.DMA((2,)),
            pltpu.SemaphoreType.DMA((2,)),
            pltpu.SemaphoreType.DMA((chips + layers + rows,)),
            pltpu.SemaphoreType.DMA((chips,)),
            pltpu.SemaphoreType.DMA((layers,)),
            pltpu.SemaphoreType.DMA((rows,)),
            pltpu.SemaphoreType.REGULAR((2, max(rows, layers))),
            pltpu.SemaphoreType.REGULAR((2, max(rows, layers))),
        ],
        compiler_params=pltpu.CompilerParams(
            collective_id=0, has_side_effects=True, vmem_limit_bytes=56 * 2**20
        ),
        name="purify",
    )(pattern, density)
    order = 2.0 * BLK * rows * columns * inners
    return purified, jnp.sum(sums, axis=1) / order


def solution(mesh):
    sizes = tuple(mesh.shape[axis] for axis in ("row", "col", "inner"))
    return jax.shard_map(
        functools.partial(on_device, sizes),
        mesh=mesh,
        in_specs=(P(("row", "col", "inner"), None), P(("row", "col", "inner"), None, None, None)),
        out_specs=(P(("row", "col", "inner"), None, None, None), P()),
        check_vma=False,
    )
```

```python
import functools

import jax
import jax.numpy as jnp
from jax import lax
from jax.experimental import pallas as pl
from jax.experimental.pallas import tpu as pltpu
from jax.sharding import PartitionSpec as P

BLK = 128
REACH = 3
SLOTS = 7
STEPS = 2
CORES = 2
MESH = pl.DeviceIdType.MESH

WINDOW = 8
COLUMNS = WINDOW + SLOTS - 1

MESSAGES = (
    (4, 0, 2, 2, 1),
    (3, 5, 2, 5, -1),
    (4, 2, 2, 2, 1),
    (3, 3, 2, 5, -1),
    (3, 0, 4, 1, 1),
    (4, 3, 4, 6, -1),
    (4, 6, 1, 2, 1),
    (2, 0, 2, 0, 1),
    (5, 5, 2, 7, -1),
    (2, 2, 2, 0, 1),
    (5, 3, 2, 7, -1),
)
PASSED = 4
FROM_OWN = ((0, 6), (1, 5), (1, 6), (2, 4), (2, 5), (5, 1), (5, 2), (6, 0), (6, 1), (7, 0))
FROM_PASSED = ((0, 5), (1, 4), (6, 2), (7, 1))
FROM_FAR = ((0, 4), (7, 2))
FROM_CROSS = ((5, 0),)


def wrapped(index, size):
    return jnp.where(index >= size, index - size, index)


def kernel(
    sizes, pattern_in, density, purified, occupation, near0, near1, left, total, square, cross, pattern,
    bit_out, bit_in, sums_a, sums_b, sums_c, send_sem, recv_sem, bit_sem, load_sem,
    sum_send, recv_a, recv_b, recv_c, in_above, in_below,
):
    rows, columns, inners = sizes
    count = rows * columns * inners
    layers = columns // CORES
    row, col, inner = lax.axis_index("row"), lax.axis_index("col"), lax.axis_index("inner")
    layer, core = lax.div(col, CORES), lax.rem(col, CORES)

    load = pltpu.make_async_copy(density, near0.at[pl.ds(3, 2)], load_sem.at[0])
    load.start()
    load_pattern = pltpu.make_async_copy(pattern_in, pattern, load_sem.at[1])
    load_pattern.start()

    after_col = jnp.where(inner == inners - 1, col + 1, col)
    before_col = jnp.where(inner == 0, col - 1, col)
    after = (
        wrapped(jnp.where(after_col == columns, row + 1, row), rows),
        wrapped(after_col, columns),
        wrapped(inner + 1, inners),
    )
    before = (
        wrapped(jnp.where(before_col < 0, row - 1, row) + rows, rows),
        wrapped(before_col + columns, columns),
        wrapped(inner + inners - 1, inners),
    )
    near_place = {1: after, -1: before}

    def chip(core_, inner_):
        return core_ * inners + inner_

    group_a = []
    for core_step in range(CORES):
        for step in range(inners):
            if core_step or step:
                core_ = wrapped(core + core_step, CORES)
                inner_ = wrapped(inner + step, inners)
                group_a.append(((row, layer * CORES + core_, inner_), chip(core_, inner_)))
    group_b = [
        ((row, wrapped(layer + step, layers) * CORES + core, inner), wrapped(layer + step, layers))
        for step in range(1, layers)
    ]
    order = sorted(range(1, rows), key=lambda step: -min(step, rows - step))
    group_c = [((wrapped(row + step, rows), col, inner), wrapped(row + step, rows)) for step in order]
    phase_a = (CORES * inners, chip(core, inner), group_a, sums_a, recv_a, 0)
    phase_b = (layers, layer, group_b, sums_b, recv_b, CORES * inners)
    phase_c = (rows, row, group_c, sums_c, recv_c, CORES * inners + layers)

    barrier = pltpu.get_barrier_semaphore()
    greeted = 0
    for place in (after, before):
        pl.semaphore_signal(barrier, inc=1, device_id=place, device_id_type=MESH)
        greeted += 1
    lines = []
    for axis, (size, at) in enumerate(
        (
            (rows, lambda step: (wrapped(row + step, rows), col, inner)),
            (layers, lambda step: (row, wrapped(layer + step, layers) * CORES + core, inner)),
        )
    ):
        if size > 1:
            lines.append((axis, size, at(1), at(size - 1)))
    greetings = [place for place, _ in group_a]
    for _, size, above, below in lines:
        greetings += [above] if size == 2 else [above, below]
    for place in greetings:
        pl.semaphore_signal(barrier, inc=1, device_id=place, device_id_type=MESH)
        greeted += 1
    zero_block = jnp.zeros((BLK, BLK), jnp.bfloat16)
    left[0:BLK, 7 * BLK : 8 * BLK] = zero_block
    left[BLK : 2 * BLK, 0:BLK] = zero_block
    left[2 * BLK : 3 * BLK, 6 * BLK : 7 * BLK] = zero_block
    left[2 * BLK : 3 * BLK, 7 * BLK : 8 * BLK] = zero_block
    load_pattern.wait()
    bit_out[...] = jnp.full((8, BLK), jnp.where(pattern[1, 2 * REACH] == 1, 1.0, 0.0), jnp.float32)
    pl.semaphore_wait(barrier, greeted)

    def spread(turn):
        for axis, size, above, below in lines:
            if turn < size // 2 - 1:
                pl.semaphore_signal(in_above.at[axis, turn], inc=1, device_id=below, device_id_type=MESH)
            if turn < (size - 1) // 2 - 1:
                pl.semaphore_signal(in_below.at[axis, turn], inc=1, device_id=above, device_id_type=MESH)

    def learn(turn):
        for axis, size, above, below in lines:
            if turn < size // 2 - 1:
                pl.semaphore_wait(in_above.at[axis, turn], 1)
            if turn < (size - 1) // 2 - 1:
                pl.semaphore_wait(in_below.at[axis, turn], 1)

    turns = max([size // 2 - 1 for _, size, _, _ in lines] + [0])

    eye = lax.broadcasted_iota(jnp.int32, (BLK, BLK), 0) == lax.broadcasted_iota(jnp.int32, (BLK, BLK), 1)

    def block(near, r, column):
        slot = column - r
        return near[r, slot] if 0 <= slot < SLOTS else zero_block

    def tile(near, r, column, width):
        return jnp.concatenate(
            [
                jnp.concatenate([block(near, r + i, column + j) for j in range(width)], axis=1)
                for i in range(2)
            ],
            axis=0,
        )

    def mirror(near, places):
        for r, slot in places:
            near[r, slot] = near[r + slot - REACH, 2 * REACH - slot].T

    def span(column, width=2):
        return slice(column * BLK, (column + width) * BLK)

    def across(a, b):
        return lax.dot_general(a, b, (((1,), (1,)), ((), ())), preferred_element_type=jnp.float32)

    def update(near, q, store):
        cube = across(square[0 : 2 * BLK, span(2 * q, 8)], tile(near, 2 * q, 2 * q, 8))
        for r in range(2):
            for j in range(2):
                slot = 2 * q + j - r
                if 0 <= slot < SLOTS:
                    mine = span(r, 1)
                    value = (
                        3.0 * square[mine, span(2 * q + j + REACH, 1)].astype(jnp.float32)
                        - 2.0 * cube[mine, span(j, 1)]
                    )
                    store(r, slot, jnp.where(pattern[r, slot] == 1, value, 0.0).astype(jnp.bfloat16))

    def exchange(section, near):
        copies = []
        for index, (r, slot, slots, target, direction) in enumerate(MESSAGES):
            source = density.at[r - 3] if section == 0 and index < 7 else near.at[r]
            copies.append(
                pltpu.make_async_remote_copy(
                    src_ref=source.at[pl.ds(slot, slots)],
                    dst_ref=near.at[target, pl.ds(slot, slots)],
                    send_sem=send_sem.at[section, index],
                    recv_sem=recv_sem.at[section, index],
                    device_id=near_place[direction],
                    device_id_type=MESH,
                )
            )
            if index < PASSED:
                copies[-1].start()
        return copies

    def follow(section, copies):
        copies[0].wait_send()
        if section == 0:
            copies[6].start()
        copies[4].start()
        copies[1].wait_send()
        copies[5].start()

    def fill_left(near):
        for r in range(2):
            for slot in range(SLOTS):
                left[span(r, 1), span(slot + r, 1)] = near[3 + r, slot]

    def relay(copies):
        for index in range(PASSED):
            copies[index].wait_recv()
            copies[index + 7].start()

    def height(section, column):
        return 3 * BLK if section == 0 and 4 <= column < 12 else 2 * BLK

    def first_half(section, near):
        mirror(near, FROM_PASSED)
        if section == 0:
            for slot in range(1, SLOTS):
                left[span(2, 1), span(slot - 1, 1)] = near[2, slot]
        for column in range(2, 12, 2):
            high = height(section, column)
            terms = [
                jnp.dot(left[0:high, span(r)], tile(near, r, column, 2), preferred_element_type=jnp.float32)
                for r in (2, 4)
                if r - 1 <= column <= r + 7
            ]
            total[0:high, span(column)] = functools.reduce(jnp.add, terms)

    def second_half(section, near, copies):
        copies[4].wait_recv()
        copies[5].wait_recv()
        mirror(near, FROM_FAR)
        if section == 0:
            learn(3)
            spread(4)
        for index in range(7, 11):
            copies[index].wait_recv()
        for column in range(0, COLUMNS, 2):
            high = height(section, column)
            terms = [total[0:high, span(column)]] if 2 <= column < 12 else []
            terms += [
                jnp.dot(left[0:high, span(r)], tile(near, r, column, 2), preferred_element_type=jnp.float32)
                for r in (0, 6)
                if r - 1 <= column <= r + 7
            ]
            value = functools.reduce(jnp.add, terms)
            if section == 0 and column == 4:
                extra = across(near[2, 0], near[2, 0])
                total[span(2, 1), span(5, 1)] = value[2 * BLK : 3 * BLK, BLK : 2 * BLK] + extra
            elif high == 3 * BLK:
                total[span(2, 1), span(column)] = value[2 * BLK : 3 * BLK]
            square[:, span(column)] = value[0 : 2 * BLK].astype(jnp.bfloat16)
        if section == 0:
            cross[...] = total[span(2, 1), span(5, 7)].astype(jnp.bfloat16)

    def send_sums(phase):
        size, me, group, sums, arrived, first = phase
        started = []
        for index, (place, _) in enumerate(group):
            copy = pltpu.make_async_remote_copy(
                src_ref=sums.at[me],
                dst_ref=sums.at[me],
                send_sem=sum_send.at[first + index],
                recv_sem=arrived.at[me],
                device_id=place,
                device_id_type=MESH,
            )
            copy.start()
            started.append(copy)
        return started

    def receive_sums(phase):
        size, me, group, sums, arrived, first = phase
        for index, (place, other) in enumerate(group):
            pltpu.make_async_remote_copy(
                src_ref=sums.at[me],
                dst_ref=sums.at[other],
                send_sem=sum_send.at[first + index],
                recv_sem=arrived.at[other],
                device_id=place,
                device_id_type=MESH,
            ).wait_recv()
        return functools.reduce(jnp.add, [sums[i] for i in range(size)])

    def down(value):
        return jnp.sum(value, axis=0, keepdims=True)

    copies0 = exchange(0, near0)
    bit = pltpu.make_async_remote_copy(
        src_ref=bit_out,
        dst_ref=bit_in,
        send_sem=bit_sem.at[0],
        recv_sem=bit_sem.at[1],
        device_id=after,
        device_id_type=MESH,
    )
    bit.start()
    spread(0)
    follow(0, copies0)
    load.wait()
    fill_left(near0)
    mirror(near0, FROM_OWN)
    learn(0)
    spread(1)
    relay(copies0)
    learn(1)
    spread(2)
    copies0[6].wait_recv()
    mirror(near0, FROM_CROSS)
    first_half(0, near0)
    learn(2)
    spread(3)
    second_half(0, near0, copies0)

    def keep(r, slot, value):
        near1[3 + r, slot] = value

    for q in range(4):
        update(near0, q, keep)
    bit.wait_recv()
    value = 3.0 * cross[:, span(3, 1)].astype(jnp.float32) - 2.0 * across(
        cross[...], jnp.concatenate([near0[5, slot] for slot in range(SLOTS)], axis=1)
    )
    near1[2, 6] = jnp.where(bit_in[0:1, :] == 1.0, value, 0.0).astype(jnp.bfloat16)
    fill_left(near1)

    sums_a[phase_a[1], 0:1] = down(
        sum(jnp.where(eye, near1[3 + r, REACH].astype(jnp.float32), 0.0) for r in range(2))
    )
    squares = sum(near1[3 + r, slot].astype(jnp.float32) ** 2 for r in range(2) for slot in range(SLOTS))
    own = left[0 : 2 * BLK, span(3)]
    outer = jnp.concatenate([left[0 : 2 * BLK, span(0, 3)], left[0 : 2 * BLK, span(5, 3)]], axis=1)
    gram = across(own, own) + 3.0 * across(outer, outer)
    cubes = own.astype(jnp.float32) * gram
    cubes = cubes[:, 0:BLK] + cubes[:, BLK : 2 * BLK]
    far = jnp.dot(left[0 : 2 * BLK, span(2, 1)], near1[2, 6], preferred_element_type=jnp.float32)
    cubes += 6.0 * far * left[0 : 2 * BLK, span(5, 1)].astype(jnp.float32)
    sums_a[phase_a[1], 1:2] = 3.0 * down(squares) - 2.0 * down(cubes)

    sent = send_sums(phase_a)
    copies1 = exchange(1, near1)
    follow(1, copies1)
    mirror(near1, FROM_OWN)
    mirror(near1, FROM_CROSS)
    sums_c[phase_c[1]] = receive_sums(phase_a)
    sent += send_sums(phase_c)
    relay(copies1)
    first_half(1, near1)
    sums_b[phase_b[1]] = receive_sums(phase_c)
    for turn in range(4, turns):
        learn(turn)
        spread(turn + 1)
    sent += send_sums(phase_b)
    second_half(1, near1, copies1)

    def finish(r, slot, value):
        purified[r, slot] = value

    for q in range(4):
        update(near1, q, finish)
    for copy in copies0[2:] + copies1[2:6] + copies1[7:] + [bit] + sent[: len(group_a) + len(group_c)]:
        copy.wait_send()
    occupation[...] = receive_sums(phase_b)
    for copy in sent[len(group_a) + len(group_c) :]:
        copy.wait_send()


def on_device(sizes, pattern, density):
    rows, columns, inners = sizes
    chips, layers = CORES * inners, columns // CORES
    flat = pltpu.VMEM((WINDOW, SLOTS, BLK, BLK), jnp.bfloat16)
    wide = COLUMNS * BLK
    purified, sums = pl.pallas_call(
        functools.partial(kernel, sizes),
        out_shape=(
            pltpu.VMEM(density.shape, jnp.bfloat16),
            pltpu.VMEM((STEPS, BLK), jnp.float32),
        ),
        in_specs=[pl.BlockSpec(memory_space=pltpu.HBM), pl.BlockSpec(memory_space=pltpu.HBM)],
        out_specs=(pl.BlockSpec(memory_space=pltpu.VMEM), pl.BlockSpec(memory_space=pltpu.VMEM)),
        scratch_shapes=[
            flat,
            flat,
            pltpu.VMEM((3 * BLK, WINDOW * BLK), jnp.bfloat16),
            pltpu.VMEM((3 * BLK, wide), jnp.float32),
            pltpu.VMEM((2 * BLK, wide), jnp.bfloat16),
            pltpu.VMEM((BLK, SLOTS * BLK), jnp.bfloat16),
            pltpu.SMEM((2, SLOTS), jnp.int32),
            pltpu.VMEM((8, BLK), jnp.float32),
            pltpu.VMEM((8, BLK), jnp.float32),
            pltpu.VMEM((chips, STEPS, BLK), jnp.float32),
            pltpu.VMEM((layers, STEPS, BLK), jnp.float32),
            pltpu.VMEM((rows, STEPS, BLK), jnp.float32),
            pltpu.SemaphoreType.DMA((STEPS, len(MESSAGES))),
            pltpu.SemaphoreType.DMA((STEPS, len(MESSAGES))),
            pltpu.SemaphoreType.DMA((2,)),
            pltpu.SemaphoreType.DMA((2,)),
            pltpu.SemaphoreType.DMA((chips + layers + rows,)),
            pltpu.SemaphoreType.DMA((chips,)),
            pltpu.SemaphoreType.DMA((layers,)),
            pltpu.SemaphoreType.DMA((rows,)),
            pltpu.SemaphoreType.REGULAR((2, max(rows, layers))),
            pltpu.SemaphoreType.REGULAR((2, max(rows, layers))),
        ],
        compiler_params=pltpu.CompilerParams(
            collective_id=0, has_side_effects=True, vmem_limit_bytes=56 * 2**20
        ),
        name="purify",
    )(pattern, density)
    order = 2.0 * BLK * rows * columns * inners
    return purified, jnp.sum(sums, axis=1) / order


def solution(mesh):
    sizes = tuple(mesh.shape[axis] for axis in ("row", "col", "inner"))
    return jax.shard_map(
        functools.partial(on_device, sizes),
        mesh=mesh,
        in_specs=(P(("row", "col", "inner"), None), P(("row", "col", "inner"), None, None, None)),
        out_specs=(P(("row", "col", "inner"), None, None, None), P()),
        check_vma=False,
    )
```

```python
import functools

import jax
import jax.numpy as jnp
from jax import lax
from jax.experimental import pallas as pl
from jax.experimental.pallas import tpu as pltpu
from jax.sharding import PartitionSpec as P

BLK = 128
REACH = 3
SLOTS = 7
STEPS = 2
CORES = 2
MESH = pl.DeviceIdType.MESH

WINDOW = 8
COLUMNS = WINDOW + SLOTS - 1

MESSAGES = (
    (4, 0, 2, 2, 1),
    (3, 5, 2, 5, -1),
    (4, 2, 2, 2, 1),
    (3, 3, 2, 5, -1),
    (3, 0, 4, 1, 1),
    (4, 3, 4, 6, -1),
    (4, 6, 1, 2, 1),
    (2, 0, 2, 0, 1),
    (5, 5, 2, 7, -1),
    (2, 2, 2, 0, 1),
    (5, 3, 2, 7, -1),
)
PASSED = 4
FROM_OWN = ((0, 6), (1, 5), (1, 6), (2, 4), (2, 5), (5, 1), (5, 2), (6, 0), (6, 1), (7, 0))
FROM_PASSED = ((0, 5), (1, 4), (6, 2), (7, 1))
FROM_FAR = ((0, 4), (7, 2))
FROM_CROSS = ((5, 0),)


def wrapped(index, size):
    return jnp.where(index >= size, index - size, index)


def kernel(
    sizes, pattern_in, density, purified, occupation, near0, near1, left, total, square, cross, pattern,
    bit_out, bit_in, sums_a, sums_b, sums_c, send_sem, recv_sem, bit_sem, load_sem,
    sum_send, recv_a, recv_b, recv_c, in_above, in_below,
):
    rows, columns, inners = sizes
    count = rows * columns * inners
    layers = columns // CORES
    row, col, inner = lax.axis_index("row"), lax.axis_index("col"), lax.axis_index("inner")
    layer, core = lax.div(col, CORES), lax.rem(col, CORES)

    load = pltpu.make_async_copy(density, near0.at[pl.ds(3, 2)], load_sem.at[0])
    load.start()
    load_pattern = pltpu.make_async_copy(pattern_in, pattern, load_sem.at[1])
    load_pattern.start()

    after_col = jnp.where(inner == inners - 1, col + 1, col)
    before_col = jnp.where(inner == 0, col - 1, col)
    after = (
        wrapped(jnp.where(after_col == columns, row + 1, row), rows),
        wrapped(after_col, columns),
        wrapped(inner + 1, inners),
    )
    before = (
        wrapped(jnp.where(before_col < 0, row - 1, row) + rows, rows),
        wrapped(before_col + columns, columns),
        wrapped(inner + inners - 1, inners),
    )
    near_place = {1: after, -1: before}

    def chip(core_, inner_):
        return core_ * inners + inner_

    group_a = []
    for core_step in range(CORES):
        for step in range(inners):
            if core_step or step:
                core_ = wrapped(core + core_step, CORES)
                inner_ = wrapped(inner + step, inners)
                group_a.append(((row, layer * CORES + core_, inner_), chip(core_, inner_)))
    group_b = [
        ((row, wrapped(layer + step, layers) * CORES + core, inner), wrapped(layer + step, layers))
        for step in range(1, layers)
    ]
    order = sorted(range(1, rows), key=lambda step: -min(step, rows - step))
    group_c = [((wrapped(row + step, rows), col, inner), wrapped(row + step, rows)) for step in order]
    phase_a = (CORES * inners, chip(core, inner), group_a, sums_a, recv_a, 0)
    phase_b = (layers, layer, group_b, sums_b, recv_b, CORES * inners)
    phase_c = (rows, row, group_c, sums_c, recv_c, CORES * inners + layers)

    barrier = pltpu.get_barrier_semaphore()
    greeted = 0
    for place in (after, before):
        pl.semaphore_signal(barrier, inc=1, device_id=place, device_id_type=MESH)
        greeted += 1
    lines = []
    for axis, (size, at) in enumerate(
        (
            (rows, lambda step: (wrapped(row + step, rows), col, inner)),
            (layers, lambda step: (row, wrapped(layer + step, layers) * CORES + core, inner)),
        )
    ):
        if size > 1:
            lines.append((axis, size, at(1), at(size - 1)))
    greetings = [place for place, _ in group_a]
    for _, size, above, below in lines:
        greetings += [above] if size == 2 else [above, below]
    for place in greetings:
        pl.semaphore_signal(barrier, inc=1, device_id=place, device_id_type=MESH)
        greeted += 1
    zero_block = jnp.zeros((BLK, BLK), jnp.bfloat16)
    left[0:BLK, 7 * BLK : 8 * BLK] = zero_block
    left[BLK : 2 * BLK, 0:BLK] = zero_block
    left[2 * BLK : 3 * BLK, 6 * BLK : 7 * BLK] = zero_block
    left[2 * BLK : 3 * BLK, 7 * BLK : 8 * BLK] = zero_block
    load_pattern.wait()
    bit_out[...] = jnp.full((8, BLK), jnp.where(pattern[1, 2 * REACH] == 1, 1.0, 0.0), jnp.float32)
    pl.semaphore_wait(barrier, greeted)

    def spread(turn):
        for axis, size, above, below in lines:
            if turn < size // 2 - 1:
                pl.semaphore_signal(in_above.at[axis, turn], inc=1, device_id=below, device_id_type=MESH)
            if turn < (size - 1) // 2 - 1:
                pl.semaphore_signal(in_below.at[axis, turn], inc=1, device_id=above, device_id_type=MESH)

    def learn(turn):
        for axis, size, above, below in lines:
            if turn < size // 2 - 1:
                pl.semaphore_wait(in_above.at[axis, turn], 1)
            if turn < (size - 1) // 2 - 1:
                pl.semaphore_wait(in_below.at[axis, turn], 1)

    turns = max([size // 2 - 1 for _, size, _, _ in lines] + [0])

    eye = lax.broadcasted_iota(jnp.int32, (BLK, BLK), 0) == lax.broadcasted_iota(jnp.int32, (BLK, BLK), 1)

    def block(near, r, column):
        slot = column - r
        return near[r, slot] if 0 <= slot < SLOTS else zero_block

    def tile(near, r, column, width):
        return jnp.concatenate(
            [
                jnp.concatenate([block(near, r + i, column + j) for j in range(width)], axis=1)
                for i in range(2)
            ],
            axis=0,
        )

    def mirror(near, places):
        for r, slot in places:
            near[r, slot] = near[r + slot - REACH, 2 * REACH - slot].T

    def span(column, width=2):
        return slice(column * BLK, (column + width) * BLK)

    def across(a, b):
        return lax.dot_general(a, b, (((1,), (1,)), ((), ())), preferred_element_type=jnp.float32)

    def update(near, q, store):
        cube = across(square[0 : 2 * BLK, span(2 * q, 8)], tile(near, 2 * q, 2 * q, 8))
        for r in range(2):
            for j in range(2):
                slot = 2 * q + j - r
                if 0 <= slot < SLOTS:
                    mine = span(r, 1)
                    value = (
                        3.0 * square[mine, span(2 * q + j + REACH, 1)].astype(jnp.float32)
                        - 2.0 * cube[mine, span(j, 1)]
                    )
                    store(r, slot, jnp.where(pattern[r, slot] == 1, value, 0.0).astype(jnp.bfloat16))

    def exchange(section, near):
        copies = []
        for index, (r, slot, slots, target, direction) in enumerate(MESSAGES):
            source = density.at[r - 3] if section == 0 and index < 7 else near.at[r]
            copies.append(
                pltpu.make_async_remote_copy(
                    src_ref=source.at[pl.ds(slot, slots)],
                    dst_ref=near.at[target, pl.ds(slot, slots)],
                    send_sem=send_sem.at[section, index],
                    recv_sem=recv_sem.at[section, index],
                    device_id=near_place[direction],
                    device_id_type=MESH,
                )
            )
            if index < PASSED:
                copies[-1].start()
        return copies

    def follow(section, copies):
        copies[0].wait_send()
        if section == 0:
            copies[6].start()
        copies[4].start()
        copies[1].wait_send()
        copies[5].start()

    def fill_left(near):
        for r in range(2):
            for slot in range(SLOTS):
                left[span(r, 1), span(slot + r, 1)] = near[3 + r, slot]

    def relay(copies):
        for index in range(PASSED):
            copies[index].wait_recv()
            copies[index + 7].start()

    def height(section, column):
        return 3 * BLK if section == 0 and 4 <= column < 12 else 2 * BLK

    def first_half(section, near):
        mirror(near, FROM_PASSED)
        if section == 0:
            for slot in range(1, SLOTS):
                left[span(2, 1), span(slot - 1, 1)] = near[2, slot]
        for column in range(2, 12, 2):
            high = height(section, column)
            terms = [
                jnp.dot(left[0:high, span(r)], tile(near, r, column, 2), preferred_element_type=jnp.float32)
                for r in (2, 4)
                if r - 1 <= column <= r + 7
            ]
            total[0:high, span(column)] = functools.reduce(jnp.add, terms)

    def second_half(section, near, copies):
        copies[4].wait_recv()
        copies[5].wait_recv()
        mirror(near, FROM_FAR)
        if section == 0:
            learn(3)
            spread(4)
        for index in range(7, 11):
            copies[index].wait_recv()
        for column in range(0, COLUMNS, 2):
            high = height(section, column)
            terms = [total[0:high, span(column)]] if 2 <= column < 12 else []
            terms += [
                jnp.dot(left[0:high, span(r)], tile(near, r, column, 2), preferred_element_type=jnp.float32)
                for r in (0, 6)
                if r - 1 <= column <= r + 7
            ]
            value = functools.reduce(jnp.add, terms)
            if section == 0 and column == 4:
                extra = across(near[2, 0], near[2, 0])
                total[span(2, 1), span(5, 1)] = value[2 * BLK : 3 * BLK, BLK : 2 * BLK] + extra
            elif high == 3 * BLK:
                total[span(2, 1), span(column)] = value[2 * BLK : 3 * BLK]
            square[:, span(column)] = value[0 : 2 * BLK].astype(jnp.bfloat16)
        if section == 0:
            cross[...] = total[span(2, 1), span(5, 7)].astype(jnp.bfloat16)

    def send_sums(phase):
        size, me, group, sums, arrived, first = phase
        started = []
        for index, (place, _) in enumerate(group):
            copy = pltpu.make_async_remote_copy(
                src_ref=sums.at[me],
                dst_ref=sums.at[me],
                send_sem=sum_send.at[first + index],
                recv_sem=arrived.at[me],
                device_id=place,
                device_id_type=MESH,
            )
            copy.start()
            started.append(copy)
        return started

    def receive_sums(phase):
        size, me, group, sums, arrived, first = phase
        for index, (place, other) in enumerate(group):
            pltpu.make_async_remote_copy(
                src_ref=sums.at[me],
                dst_ref=sums.at[other],
                send_sem=sum_send.at[first + index],
                recv_sem=arrived.at[other],
                device_id=place,
                device_id_type=MESH,
            ).wait_recv()
        return functools.reduce(jnp.add, [sums[i] for i in range(size)])

    def down(value):
        return jnp.sum(value, axis=0, keepdims=True)

    copies0 = exchange(0, near0)
    bit = pltpu.make_async_remote_copy(
        src_ref=bit_out,
        dst_ref=bit_in,
        send_sem=bit_sem.at[0],
        recv_sem=bit_sem.at[1],
        device_id=after,
        device_id_type=MESH,
    )
    bit.start()
    spread(0)
    follow(0, copies0)
    load.wait()
    fill_left(near0)
    mirror(near0, FROM_OWN)
    learn(0)
    spread(1)
    relay(copies0)
    learn(1)
    spread(2)
    copies0[6].wait_recv()
    mirror(near0, FROM_CROSS)
    first_half(0, near0)
    learn(2)
    spread(3)
    second_half(0, near0, copies0)

    def keep(r, slot, value):
        near1[3 + r, slot] = value

    for q in range(4):
        update(near0, q, keep)
    bit.wait_recv()
    value = 3.0 * cross[:, span(3, 1)].astype(jnp.float32) - 2.0 * across(
        cross[...], jnp.concatenate([near0[5, slot] for slot in range(SLOTS)], axis=1)
    )
    near1[2, 6] = jnp.where(bit_in[0:1, :] == 1.0, value, 0.0).astype(jnp.bfloat16)
    fill_left(near1)

    sums_a[phase_a[1], 0:1] = down(
        sum(jnp.where(eye, near1[3 + r, REACH].astype(jnp.float32), 0.0) for r in range(2))
    )
    squares = sum(near1[3 + r, slot].astype(jnp.float32) ** 2 for r in range(2) for slot in range(SLOTS))
    own = left[0 : 2 * BLK, span(3)]
    outer = jnp.concatenate([left[0 : 2 * BLK, span(0, 3)], left[0 : 2 * BLK, span(5, 3)]], axis=1)
    gram = across(own, own) + 3.0 * across(outer, outer)
    cubes = own.astype(jnp.float32) * gram
    cubes = cubes[:, 0:BLK] + cubes[:, BLK : 2 * BLK]
    far = jnp.dot(left[0 : 2 * BLK, span(2, 1)], near1[2, 6], preferred_element_type=jnp.float32)
    cubes += 6.0 * far * left[0 : 2 * BLK, span(5, 1)].astype(jnp.float32)
    sums_a[phase_a[1], 1:2] = 3.0 * down(squares) - 2.0 * down(cubes)

    sent = send_sums(phase_a)
    copies1 = exchange(1, near1)
    follow(1, copies1)
    mirror(near1, FROM_OWN)
    mirror(near1, FROM_CROSS)
    sums_c[phase_c[1]] = receive_sums(phase_a)
    sent += send_sums(phase_c)
    relay(copies1)
    sums_b[phase_b[1]] = receive_sums(phase_c)
    for turn in range(4, turns):
        learn(turn)
        spread(turn + 1)
    sent += send_sums(phase_b)
    first_half(1, near1)
    second_half(1, near1, copies1)

    def finish(r, slot, value):
        purified[r, slot] = value

    for q in range(4):
        update(near1, q, finish)
    for copy in copies0[2:] + copies1[2:6] + copies1[7:] + [bit] + sent[: len(group_a) + len(group_c)]:
        copy.wait_send()
    occupation[...] = receive_sums(phase_b)
    for copy in sent[len(group_a) + len(group_c) :]:
        copy.wait_send()


def on_device(sizes, pattern, density):
    rows, columns, inners = sizes
    chips, layers = CORES * inners, columns // CORES
    flat = pltpu.VMEM((WINDOW, SLOTS, BLK, BLK), jnp.bfloat16)
    wide = COLUMNS * BLK
    purified, sums = pl.pallas_call(
        functools.partial(kernel, sizes),
        out_shape=(
            pltpu.VMEM(density.shape, jnp.bfloat16),
            pltpu.VMEM((STEPS, BLK), jnp.float32),
        ),
        in_specs=[pl.BlockSpec(memory_space=pltpu.HBM), pl.BlockSpec(memory_space=pltpu.HBM)],
        out_specs=(pl.BlockSpec(memory_space=pltpu.VMEM), pl.BlockSpec(memory_space=pltpu.VMEM)),
        scratch_shapes=[
            flat,
            flat,
            pltpu.VMEM((3 * BLK, WINDOW * BLK), jnp.bfloat16),
            pltpu.VMEM((3 * BLK, wide), jnp.float32),
            pltpu.VMEM((2 * BLK, wide), jnp.bfloat16),
            pltpu.VMEM((BLK, SLOTS * BLK), jnp.bfloat16),
            pltpu.SMEM((2, SLOTS), jnp.int32),
            pltpu.VMEM((8, BLK), jnp.float32),
            pltpu.VMEM((8, BLK), jnp.float32),
            pltpu.VMEM((chips, STEPS, BLK), jnp.float32),
            pltpu.VMEM((layers, STEPS, BLK), jnp.float32),
            pltpu.VMEM((rows, STEPS, BLK), jnp.float32),
            pltpu.SemaphoreType.DMA((STEPS, len(MESSAGES))),
            pltpu.SemaphoreType.DMA((STEPS, len(MESSAGES))),
            pltpu.SemaphoreType.DMA((2,)),
            pltpu.SemaphoreType.DMA((2,)),
            pltpu.SemaphoreType.DMA((chips + layers + rows,)),
            pltpu.SemaphoreType.DMA((chips,)),
            pltpu.SemaphoreType.DMA((layers,)),
            pltpu.SemaphoreType.DMA((rows,)),
            pltpu.SemaphoreType.REGULAR((2, max(rows, layers))),
            pltpu.SemaphoreType.REGULAR((2, max(rows, layers))),
        ],
        compiler_params=pltpu.CompilerParams(
            collective_id=0, has_side_effects=True, vmem_limit_bytes=56 * 2**20
        ),
        name="purify",
    )(pattern, density)
    order = 2.0 * BLK * rows * columns * inners
    return purified, jnp.sum(sums, axis=1) / order


def solution(mesh):
    sizes = tuple(mesh.shape[axis] for axis in ("row", "col", "inner"))
    return jax.shard_map(
        functools.partial(on_device, sizes),
        mesh=mesh,
        in_specs=(P(("row", "col", "inner"), None), P(("row", "col", "inner"), None, None, None)),
        out_specs=(P(("row", "col", "inner"), None, None, None), P()),
        check_vma=False,
    )
```

```python
import functools

import jax
import jax.numpy as jnp
from jax import lax
from jax.experimental import pallas as pl
from jax.experimental.pallas import tpu as pltpu
from jax.sharding import PartitionSpec as P

BLK = 128
REACH = 3
SLOTS = 7
STEPS = 2
CORES = 2
MESH = pl.DeviceIdType.MESH

WINDOW = 8
COLUMNS = WINDOW + SLOTS - 1

MESSAGES = (
    (4, 0, 1, 2, 1),
    (3, 6, 1, 5, -1),
    (4, 1, 3, 2, 1),
    (3, 3, 3, 5, -1),
    (3, 0, 4, 1, 1),
    (4, 3, 4, 6, -1),
    (4, 6, 1, 2, 1),
    (2, 0, 1, 0, 1),
    (5, 6, 1, 7, -1),
    (2, 1, 3, 0, 1),
    (5, 3, 3, 7, -1),
)
PASSED = 4
FROM_OWN = ((0, 6), (1, 5), (1, 6), (2, 4), (2, 5), (5, 1), (5, 2), (6, 0), (6, 1), (7, 0))
FROM_PASSED = ((0, 5), (1, 4), (6, 2), (7, 1))
FROM_FAR = ((0, 4), (7, 2))
FROM_CROSS = ((5, 0),)


def wrapped(index, size):
    return jnp.where(index >= size, index - size, index)


def kernel(
    sizes, pattern_in, density, purified, occupation, near0, near1, left, total, square, cross, pattern,
    bit_out, bit_in, sums_a, sums_b, sums_c, send_sem, recv_sem, bit_sem, load_sem,
    sum_send, recv_a, recv_b, recv_c, in_above, in_below,
):
    rows, columns, inners = sizes
    count = rows * columns * inners
    layers = columns // CORES
    row, col, inner = lax.axis_index("row"), lax.axis_index("col"), lax.axis_index("inner")
    layer, core = lax.div(col, CORES), lax.rem(col, CORES)

    load = pltpu.make_async_copy(density, near0.at[pl.ds(3, 2)], load_sem.at[0])
    load.start()
    load_pattern = pltpu.make_async_copy(pattern_in, pattern, load_sem.at[1])
    load_pattern.start()

    after_col = jnp.where(inner == inners - 1, col + 1, col)
    before_col = jnp.where(inner == 0, col - 1, col)
    after = (
        wrapped(jnp.where(after_col == columns, row + 1, row), rows),
        wrapped(after_col, columns),
        wrapped(inner + 1, inners),
    )
    before = (
        wrapped(jnp.where(before_col < 0, row - 1, row) + rows, rows),
        wrapped(before_col + columns, columns),
        wrapped(inner + inners - 1, inners),
    )
    near_place = {1: after, -1: before}

    def chip(core_, inner_):
        return core_ * inners + inner_

    group_a = []
    for core_step in range(CORES):
        for step in range(inners):
            if core_step or step:
                core_ = wrapped(core + core_step, CORES)
                inner_ = wrapped(inner + step, inners)
                group_a.append(((row, layer * CORES + core_, inner_), chip(core_, inner_)))
    group_b = [
        ((row, wrapped(layer + step, layers) * CORES + core, inner), wrapped(layer + step, layers))
        for step in range(1, layers)
    ]
    order = sorted(range(1, rows), key=lambda step: -min(step, rows - step))
    group_c = [((wrapped(row + step, rows), col, inner), wrapped(row + step, rows)) for step in order]
    phase_a = (CORES * inners, chip(core, inner), group_a, sums_a, recv_a, 0)
    phase_b = (layers, layer, group_b, sums_b, recv_b, CORES * inners)
    phase_c = (rows, row, group_c, sums_c, recv_c, CORES * inners + layers)

    barrier = pltpu.get_barrier_semaphore()
    greeted = 0
    for place in (after, before):
        pl.semaphore_signal(barrier, inc=1, device_id=place, device_id_type=MESH)
        greeted += 1
    lines = []
    for axis, (size, at) in enumerate(
        (
            (rows, lambda step: (wrapped(row + step, rows), col, inner)),
            (layers, lambda step: (row, wrapped(layer + step, layers) * CORES + core, inner)),
        )
    ):
        if size > 1:
            lines.append((axis, size, at(1), at(size - 1)))
    greetings = [place for place, _ in group_a]
    for _, size, above, below in lines:
        greetings += [above] if size == 2 else [above, below]
    for place in greetings:
        pl.semaphore_signal(barrier, inc=1, device_id=place, device_id_type=MESH)
        greeted += 1
    zero_block = jnp.zeros((BLK, BLK), jnp.bfloat16)
    left[0:BLK, 7 * BLK : 8 * BLK] = zero_block
    left[BLK : 2 * BLK, 0:BLK] = zero_block
    left[2 * BLK : 3 * BLK, 6 * BLK : 7 * BLK] = zero_block
    left[2 * BLK : 3 * BLK, 7 * BLK : 8 * BLK] = zero_block
    load_pattern.wait()
    bit_out[...] = jnp.full((8, BLK), jnp.where(pattern[1, 2 * REACH] == 1, 1.0, 0.0), jnp.float32)
    pl.semaphore_wait(barrier, greeted)

    def spread(turn):
        for axis, size, above, below in lines:
            if turn < size // 2 - 1:
                pl.semaphore_signal(in_above.at[axis, turn], inc=1, device_id=below, device_id_type=MESH)
            if turn < (size - 1) // 2 - 1:
                pl.semaphore_signal(in_below.at[axis, turn], inc=1, device_id=above, device_id_type=MESH)

    def learn(turn):
        for axis, size, above, below in lines:
            if turn < size // 2 - 1:
                pl.semaphore_wait(in_above.at[axis, turn], 1)
            if turn < (size - 1) // 2 - 1:
                pl.semaphore_wait(in_below.at[axis, turn], 1)

    turns = max([size // 2 - 1 for _, size, _, _ in lines] + [0])

    eye = lax.broadcasted_iota(jnp.int32, (BLK, BLK), 0) == lax.broadcasted_iota(jnp.int32, (BLK, BLK), 1)

    def block(near, r, column):
        slot = column - r
        return near[r, slot] if 0 <= slot < SLOTS else zero_block

    def tile(near, r, column, width):
        return jnp.concatenate(
            [
                jnp.concatenate([block(near, r + i, column + j) for j in range(width)], axis=1)
                for i in range(2)
            ],
            axis=0,
        )

    def mirror(near, places):
        for r, slot in places:
            near[r, slot] = near[r + slot - REACH, 2 * REACH - slot].T

    def span(column, width=2):
        return slice(column * BLK, (column + width) * BLK)

    def across(a, b):
        return lax.dot_general(a, b, (((1,), (1,)), ((), ())), preferred_element_type=jnp.float32)

    def update(near, q, store):
        cube = across(square[0 : 2 * BLK, span(2 * q, 8)], tile(near, 2 * q, 2 * q, 8))
        for r in range(2):
            for j in range(2):
                slot = 2 * q + j - r
                if 0 <= slot < SLOTS:
                    mine = span(r, 1)
                    value = (
                        3.0 * square[mine, span(2 * q + j + REACH, 1)].astype(jnp.float32)
                        - 2.0 * cube[mine, span(j, 1)]
                    )
                    store(r, slot, jnp.where(pattern[r, slot] == 1, value, 0.0).astype(jnp.bfloat16))

    def exchange(section, near):
        copies = []
        for index, (r, slot, slots, target, direction) in enumerate(MESSAGES):
            source = density.at[r - 3] if section == 0 and index < 7 else near.at[r]
            copies.append(
                pltpu.make_async_remote_copy(
                    src_ref=source.at[pl.ds(slot, slots)],
                    dst_ref=near.at[target, pl.ds(slot, slots)],
                    send_sem=send_sem.at[section, index],
                    recv_sem=recv_sem.at[section, index],
                    device_id=near_place[direction],
                    device_id_type=MESH,
                )
            )
            if index < PASSED:
                copies[-1].start()
        return copies

    def follow(section, copies):
        copies[0].wait_send()
        if section == 0:
            copies[6].start()
        copies[4].start()
        copies[1].wait_send()
        copies[5].start()

    def fill_left(near):
        for r in range(2):
            for slot in range(SLOTS):
                left[span(r, 1), span(slot + r, 1)] = near[3 + r, slot]

    def relay(copies):
        for index in range(PASSED):
            copies[index].wait_recv()
            copies[index + 7].start()

    def height(section, column):
        return 3 * BLK if section == 0 and 4 <= column < 12 else 2 * BLK

    def first_half(section, near):
        mirror(near, FROM_PASSED)
        if section == 0:
            for slot in range(1, SLOTS):
                left[span(2, 1), span(slot - 1, 1)] = near[2, slot]
        for column in range(2, 12, 2):
            high = height(section, column)
            terms = [
                jnp.dot(left[0:high, span(r)], tile(near, r, column, 2), preferred_element_type=jnp.float32)
                for r in (2, 4)
                if r - 1 <= column <= r + 7
            ]
            total[0:high, span(column)] = functools.reduce(jnp.add, terms)

    def second_half(section, near, copies):
        copies[4].wait_recv()
        copies[5].wait_recv()
        mirror(near, FROM_FAR)
        if section == 0:
            learn(3)
            spread(4)
        for index in range(7, 11):
            copies[index].wait_recv()
        for column in range(0, COLUMNS, 2):
            high = height(section, column)
            terms = [total[0:high, span(column)]] if 2 <= column < 12 else []
            terms += [
                jnp.dot(left[0:high, span(r)], tile(near, r, column, 2), preferred_element_type=jnp.float32)
                for r in (0, 6)
                if r - 1 <= column <= r + 7
            ]
            value = functools.reduce(jnp.add, terms)
            if section == 0 and column == 4:
                extra = across(near[2, 0], near[2, 0])
                total[span(2, 1), span(5, 1)] = value[2 * BLK : 3 * BLK, BLK : 2 * BLK] + extra
            elif high == 3 * BLK:
                total[span(2, 1), span(column)] = value[2 * BLK : 3 * BLK]
            square[:, span(column)] = value[0 : 2 * BLK].astype(jnp.bfloat16)
        if section == 0:
            cross[...] = total[span(2, 1), span(5, 7)].astype(jnp.bfloat16)

    def send_sums(phase):
        size, me, group, sums, arrived, first = phase
        started = []
        for index, (place, _) in enumerate(group):
            copy = pltpu.make_async_remote_copy(
                src_ref=sums.at[me],
                dst_ref=sums.at[me],
                send_sem=sum_send.at[first + index],
                recv_sem=arrived.at[me],
                device_id=place,
                device_id_type=MESH,
            )
            copy.start()
            started.append(copy)
        return started

    def receive_sums(phase):
        size, me, group, sums, arrived, first = phase
        for index, (place, other) in enumerate(group):
            pltpu.make_async_remote_copy(
                src_ref=sums.at[me],
                dst_ref=sums.at[other],
                send_sem=sum_send.at[first + index],
                recv_sem=arrived.at[other],
                device_id=place,
                device_id_type=MESH,
            ).wait_recv()
        return functools.reduce(jnp.add, [sums[i] for i in range(size)])

    def down(value):
        return jnp.sum(value, axis=0, keepdims=True)

    copies0 = exchange(0, near0)
    bit = pltpu.make_async_remote_copy(
        src_ref=bit_out,
        dst_ref=bit_in,
        send_sem=bit_sem.at[0],
        recv_sem=bit_sem.at[1],
        device_id=after,
        device_id_type=MESH,
    )
    bit.start()
    spread(0)
    follow(0, copies0)
    load.wait()
    fill_left(near0)
    mirror(near0, FROM_OWN)
    learn(0)
    spread(1)
    relay(copies0)
    learn(1)
    spread(2)
    copies0[6].wait_recv()
    mirror(near0, FROM_CROSS)
    first_half(0, near0)
    learn(2)
    spread(3)
    second_half(0, near0, copies0)

    def keep(r, slot, value):
        near1[3 + r, slot] = value

    for q in range(4):
        update(near0, q, keep)
    bit.wait_recv()
    value = 3.0 * cross[:, span(3, 1)].astype(jnp.float32) - 2.0 * across(
        cross[...], jnp.concatenate([near0[5, slot] for slot in range(SLOTS)], axis=1)
    )
    near1[2, 6] = jnp.where(bit_in[0:1, :] == 1.0, value, 0.0).astype(jnp.bfloat16)
    fill_left(near1)

    sums_a[phase_a[1], 0:1] = down(
        sum(jnp.where(eye, near1[3 + r, REACH].astype(jnp.float32), 0.0) for r in range(2))
    )
    squares = sum(near1[3 + r, slot].astype(jnp.float32) ** 2 for r in range(2) for slot in range(SLOTS))
    own = left[0 : 2 * BLK, span(3)]
    outer = jnp.concatenate([left[0 : 2 * BLK, span(0, 3)], left[0 : 2 * BLK, span(5, 3)]], axis=1)
    gram = across(own, own) + 3.0 * across(outer, outer)
    cubes = own.astype(jnp.float32) * gram
    cubes = cubes[:, 0:BLK] + cubes[:, BLK : 2 * BLK]
    far = jnp.dot(left[0 : 2 * BLK, span(2, 1)], near1[2, 6], preferred_element_type=jnp.float32)
    cubes += 6.0 * far * left[0 : 2 * BLK, span(5, 1)].astype(jnp.float32)
    sums_a[phase_a[1], 1:2] = 3.0 * down(squares) - 2.0 * down(cubes)

    sent = send_sums(phase_a)
    copies1 = exchange(1, near1)
    follow(1, copies1)
    mirror(near1, FROM_OWN)
    mirror(near1, FROM_CROSS)
    sums_c[phase_c[1]] = receive_sums(phase_a)
    sent += send_sums(phase_c)
    relay(copies1)
    first_half(1, near1)
    sums_b[phase_b[1]] = receive_sums(phase_c)
    for turn in range(4, turns):
        learn(turn)
        spread(turn + 1)
    sent += send_sums(phase_b)
    second_half(1, near1, copies1)

    def finish(r, slot, value):
        purified[r, slot] = value

    for q in range(4):
        update(near1, q, finish)
    for copy in copies0[2:] + copies1[2:6] + copies1[7:] + [bit] + sent[: len(group_a) + len(group_c)]:
        copy.wait_send()
    occupation[...] = receive_sums(phase_b)
    for copy in sent[len(group_a) + len(group_c) :]:
        copy.wait_send()


def on_device(sizes, pattern, density):
    rows, columns, inners = sizes
    chips, layers = CORES * inners, columns // CORES
    flat = pltpu.VMEM((WINDOW, SLOTS, BLK, BLK), jnp.bfloat16)
    wide = COLUMNS * BLK
    purified, sums = pl.pallas_call(
        functools.partial(kernel, sizes),
        out_shape=(
            pltpu.VMEM(density.shape, jnp.bfloat16),
            pltpu.VMEM((STEPS, BLK), jnp.float32),
        ),
        in_specs=[pl.BlockSpec(memory_space=pltpu.HBM), pl.BlockSpec(memory_space=pltpu.HBM)],
        out_specs=(pl.BlockSpec(memory_space=pltpu.VMEM), pl.BlockSpec(memory_space=pltpu.VMEM)),
        scratch_shapes=[
            flat,
            flat,
            pltpu.VMEM((3 * BLK, WINDOW * BLK), jnp.bfloat16),
            pltpu.VMEM((3 * BLK, wide), jnp.float32),
            pltpu.VMEM((2 * BLK, wide), jnp.bfloat16),
            pltpu.VMEM((BLK, SLOTS * BLK), jnp.bfloat16),
            pltpu.SMEM((2, SLOTS), jnp.int32),
            pltpu.VMEM((8, BLK), jnp.float32),
            pltpu.VMEM((8, BLK), jnp.float32),
            pltpu.VMEM((chips, STEPS, BLK), jnp.float32),
            pltpu.VMEM((layers, STEPS, BLK), jnp.float32),
            pltpu.VMEM((rows, STEPS, BLK), jnp.float32),
            pltpu.SemaphoreType.DMA((STEPS, len(MESSAGES))),
            pltpu.SemaphoreType.DMA((STEPS, len(MESSAGES))),
            pltpu.SemaphoreType.DMA((2,)),
            pltpu.SemaphoreType.DMA((2,)),
            pltpu.SemaphoreType.DMA((chips + layers + rows,)),
            pltpu.SemaphoreType.DMA((chips,)),
            pltpu.SemaphoreType.DMA((layers,)),
            pltpu.SemaphoreType.DMA((rows,)),
            pltpu.SemaphoreType.REGULAR((2, max(rows, layers))),
            pltpu.SemaphoreType.REGULAR((2, max(rows, layers))),
        ],
        compiler_params=pltpu.CompilerParams(
            collective_id=0, has_side_effects=True, vmem_limit_bytes=56 * 2**20
        ),
        name="purify",
    )(pattern, density)
    order = 2.0 * BLK * rows * columns * inners
    return purified, jnp.sum(sums, axis=1) / order


def solution(mesh):
    sizes = tuple(mesh.shape[axis] for axis in ("row", "col", "inner"))
    return jax.shard_map(
        functools.partial(on_device, sizes),
        mesh=mesh,
        in_specs=(P(("row", "col", "inner"), None), P(("row", "col", "inner"), None, None, None)),
        out_specs=(P(("row", "col", "inner"), None, None, None), P()),
        check_vma=False,
    )
```
